32 devices in a mesh: row: 8 (over y, x, core), col: 4 (over z).
Axes of the slice: x: 2, y: 2, z: 4, core: 2. Of those that a mesh axis runs over, the one named last changes fastest.
Arguments:
- slab_embed: float32 [16384, 768], P(('col', 'row')), may hold values from -1 to 1
- coverage_old: float32 [16384], P('col'), may hold values from 2 to 4.5
- sel_index: int32 [1024], P('row'), may hold values from 0 to 16383
- cand_index: int32 [1536], P('row'), may hold values from 0 to 16383
Outputs:
- coverage: float32 [16384], P('col')
- total_gain: float32 [1536], P('row')
The draws below stay inside these ranges and needn't reach their ends.
Inputs may be any that keep to these rules, and one draw needn't show every extreme that they name: `sel_index`: indices into the slab. `cand_index`: indices into the slab.
All inputs are finite; a program needn't handle non-finite values.
Results may differ from the reference program's by a relative error of at most 0.00014.
Values sent between devices are 32-bit elements; how exact they have to be, the bound alone decides.
A program may use at most 128 MiB of HBM per device.

```python
import jax
import jax.numpy as jnp
from jax import lax

D = 768
N = 16384
K = 1536
S = 1024
N_COL = 4


def plant(array, key, low, largest):
    longest = array.shape.index(max(array.shape))
    spots = []
    for shift in (0, 1):
        where = [jax.random.randint(jax.random.fold_in(key, axis), (), 0, length) for axis, length in enumerate(array.shape)]
        where[longest] = (where[longest] + shift) % array.shape[longest]
        spots.append(tuple(where))
    return array.at[spots[0]].set(low).at[spots[1]].set(largest)


def levels(stream_key, dims, cuts, low, top_value):
    level, own = 1.0, jax.random.fold_in(stream_key, 6)
    for axis_at, parts in cuts:
        steps = jnp.exp(jax.random.uniform(jax.random.fold_in(own, axis_at), (parts,), jnp.float32, low / len(cuts), top_value / len(cuts)))
        level = level * jnp.repeat(steps, dims[axis_at] // parts).reshape([-1 if axis == axis_at else 1 for axis in range(len(dims))])
    return level


def noise(key, dims, deviation, limit, split=(), held_as=jnp.bfloat16):
    entries = deviation * jax.random.normal(key, dims, jnp.float32)
    if split:
        entries = entries * levels(key, dims, split, -0.22, 0.18)
    return jnp.clip(entries, -limit, limit).astype(held_as)


def setup_inputs(seed: int = 0) -> dict:
    splits = jax.random.split(jax.random.key(seed), 5)
    slab_embed = noise(splits[0], (N, D), 0.19, 1.0, ((0, 32),), jnp.float32)
    coverage_old = jnp.clip(2.0 + 2.5 * jax.random.uniform(splits[1], (N,), jnp.float32) ** levels(splits[1], (N,), ((0, 4),), -0.2, 0.2), 2.0, 4.5)
    sel_index = plant(jax.random.randint(splits[2], (S,), 0, N), jax.random.fold_in(splits[2], 1), 0, N - 1).astype(jnp.int32)
    cand_index = plant(jax.random.randint(splits[3], (K,), 0, N), jax.random.fold_in(splits[3], 1), 0, N - 1).astype(jnp.int32)
    return {"slab_embed": slab_embed, "coverage_old": coverage_old, "sel_index": sel_index, "cand_index": cand_index}


def similar(left, right):
    return lax.dot_general(left, right, (((1,), (1,)), ((), ())), precision=lax.Precision.HIGHEST, preferred_element_type=jnp.float32)


def reference(slab_embed, coverage_old, sel_index, cand_index):
    selected = jnp.take(slab_embed, sel_index, axis=0)
    chosen = jnp.take(slab_embed, cand_index, axis=0)
    blocks = slab_embed.reshape(N_COL, -1, D)
    old_blocks = coverage_old.reshape(N_COL, -1)

    def per_block(packed):
        points, previous = packed
        reached = jnp.max(similar(selected, points), axis=0)
        updated = jnp.maximum(previous, reached)
        scores = similar(chosen, points)
        return updated, jnp.sum(jnp.maximum(scores - updated[None, :], 0.0), axis=1)

    covered, partial_value = lax.map(per_block, (blocks, old_blocks))
    return covered.reshape(-1), jnp.sum(partial_value, axis=0)
```

```python
import functools

import jax
import jax.numpy as jnp
from jax import lax
from jax.experimental import pallas as pl
from jax.experimental.pallas import tpu as pltpu
from jax.sharding import PartitionSpec as P

MESH = pl.DeviceIdType.MESH
QUAD = 4
NT = (((1,), (1,)), ((), ()))


def similar(left, right):
    return lax.dot_general(
        left,
        right,
        (((1,), (1,)), ((), ())),
        precision=lax.Precision.HIGHEST,
        preferred_element_type=jnp.float32,
    )


def lookup(source, indices, first_row):
    position = indices - first_row
    inside = (position >= 0) & (position < source.shape[0])
    picked = jnp.take(source, jnp.clip(position, 0, source.shape[0] - 1), axis=0)
    return jnp.where(inside[:, None], picked, 0.0)


def any_draw(slab_embed, coverage_old, sel_index, cand_index):
    col_id = lax.axis_index("col")
    gathered = lax.all_gather(slab_embed, "row", axis=0, tiled=True)
    first_row = col_id * gathered.shape[0]
    selected, chosen = lax.psum(
        (lookup(gathered, sel_index, first_row), lookup(gathered, cand_index, first_row)), "col"
    )
    partial_value = jnp.max(similar(selected, gathered), axis=0)
    reached = lax.pmax(partial_value, "row")
    coverage = jnp.maximum(coverage_old, reached)
    gain_part = jnp.sum(jnp.maximum(similar(chosen, gathered) - coverage[None, :], 0.0), axis=1)
    return coverage, lax.psum(gain_part, "col")


def halves(value):
    high = value.astype(jnp.bfloat16)
    return high, (value - high.astype(jnp.float32)).astype(jnp.bfloat16)


def dot_nt(left, right):
    return lax.dot_general(left, right, NT, preferred_element_type=jnp.float32)


def kernel(
    R, C, cap, slab, cov_old, sel, cand, cand_col,
    cov_out, gain_out, flag_out,
    pts, ph, plo, qs, qh, ql, sc, idx, mx, cov, gp, gr,
    idx_send, idx_recv, core_send, core_recv, x_send, x_recv, f_send, f_recv,
    q_recv, ql_send, qr_send, qa_send, m_send, m_recv, c_send, c_recv, g_send, g_recv,
):
    A = R // QUAD
    NB = A * C
    ND = R * C
    rows = slab.shape[0]
    ns, nk = sel.shape[1], cand.shape[1]
    shift = rows.bit_length() - 1
    span = QUAD * rows
    r = lax.axis_index("row")
    c = lax.axis_index("col")
    me = c * R + r
    a = r // QUAD
    m = r % QUAD
    x, h = m // 2, m % 2
    m_core = 2 * x + (1 - h)
    m_x = 2 * (1 - x) + h
    m_diag = 2 * (1 - x) + (1 - h)
    base = a * QUAD
    chunk = rows // C

    def remote(src, dst, ssem, rsem, row, col):
        return pltpu.make_async_remote_copy(
            src_ref=src, dst_ref=dst, send_sem=ssem, recv_sem=rsem,
            device_id=(row, col), device_id_type=MESH,
        )

    barrier = pltpu.get_barrier_semaphore()

    def greet(i, carry):
        dev = (me + i) % ND
        pl.semaphore_signal(barrier, inc=1, device_id=(dev % R, dev // R), device_id_type=MESH)
        return carry

    lax.fori_loop(1, ND, greet, 0)
    idx[r, :, 0:ns] = sel[...]
    idx[r, :, ns : ns + nk] = cand[...]
    pl.semaphore_wait(barrier, ND - 1)

    def idx_copy(slot, to):
        return remote(idx.at[slot], idx.at[slot], idx_send.at[to], idx_recv.at[slot], to, c)

    for i in range(1, R):
        idx_copy(r, (r + i) % R).start()

    core_copy = remote(slab, pts.at[m], core_send.at[0], core_recv.at[0], base + m_core, c)
    core_copy.start()

    def x_copy(s):
        part = pl.ds(s * chunk, chunk)
        return remote(slab.at[part], pts.at[m, part], x_send.at[s], x_recv.at[s], base + m_x, c)

    def x_landed(s):
        part = pl.ds(s * chunk, chunk)
        return remote(slab.at[part], pts.at[m_x, part], x_send.at[s], x_recv.at[s], base + m_x, c)

    def f_copy(s):
        part = pl.ds(s * chunk, chunk)
        return remote(pts.at[m_x, part], pts.at[m_x, part], f_send.at[s], f_recv.at[s], base + m_core, c)

    def f_landed(s):
        part = pl.ds(s * chunk, chunk)
        return remote(pts.at[m_diag, part], pts.at[m_diag, part], f_send.at[s], f_recv.at[s], base + m_core, c)

    for s in range(C):
        x_copy(s).start()

    def split_points(source, slot):
        for part in range(0, rows, 256):
            high, low = halves(source[part : part + 256])
            ph[slot, part : part + 256] = high
            plo[slot, part : part + 256] = low

    split_points(slab, m)

    for i in range(1, R):
        idx_copy((r + i) % R, (r + i) % R).wait_recv()

    everything = jnp.concatenate([idx[j] for j in range(R)], axis=0)
    owner = lax.shift_right_logical(everything, shift)
    local = (everything - owner * rows).astype(jnp.float32)
    owner_sel, owner_cand = owner[:, 0:ns], owner[:, ns : ns + nk]

    def ranks(mask):
        n = mask.shape[1]
        before = lax.broadcasted_iota(jnp.int32, (n, n), 0) < lax.broadcasted_iota(jnp.int32, (n, n), 1)
        return jnp.dot(
            mask.astype(jnp.bfloat16), before.astype(jnp.bfloat16), preferred_element_type=jnp.float32
        )

    def place(owners, locals_, start, packed):
        mask = jnp.where(owners == me, 1.0, 0.0)
        within = ranks(mask)
        slot = lax.broadcasted_iota(jnp.int32, (cap, mask.shape[1]), 0).astype(jnp.float32)
        for j in range(R):
            rank = jnp.where(mask[j : j + 1] > 0.0, within[j : j + 1] + start, -1.0)
            packed = packed + jnp.sum(
                jnp.where(rank == slot, locals_[j : j + 1] + 1.0, 0.0), axis=1, keepdims=True
            )
            start = start + jnp.sum(mask[j : j + 1], axis=1, keepdims=True)
        return start, packed

    start, packed = place(owner_sel, local[:, 0:ns], jnp.zeros((1, 1), jnp.float32), jnp.zeros((cap, 1), jnp.float32))
    start, packed = place(owner_cand, local[:, ns : ns + nk], start, packed)
    point = lax.broadcasted_iota(jnp.int32, (cap, rows), 1).astype(jnp.float32)
    pick = jnp.where(point == packed - 1.0, 1.0, 0.0)
    own = a * C + c
    qs[own] = jnp.dot(pick, slab[...], precision=lax.Precision.HIGHEST, preferred_element_type=jnp.float32)

    def q_copy(b, ssem, row, col):
        return remote(qs.at[b], qs.at[b], ssem.at[b], q_recv.at[b], row, col)

    def q_right(b):
        return q_copy(b, qr_send, r, c + 1)

    def q_left(b):
        return q_copy(b, ql_send, r, c - 1)

    def q_across(b, i):
        return q_copy(b, qa_send.at[i - 1], ((a + i) % A) * QUAD + m, c)

    def spread(b):
        for i in range(1, A):
            q_across(b, i).start()

    @pl.when(c + 1 < C)
    def _():
        q_right(own).start()

    @pl.when(c > 0)
    def _():
        q_left(own).start()

    spread(own)

    def split_block(b):
        high, low = halves(qs[b])
        qh[pl.ds(b * cap, cap)] = high
        ql[pl.ds(b * cap, cap)] = low

    width = 256

    def near_scores(b):
        split_block(b)

        def step(t, carry):
            slot = 2 * x + t // (rows // width)
            part = pl.ds((t % (rows // width)) * width, width)
            high, low = ph[slot, part], plo[slot, part]
            q1, q2 = qh[pl.ds(b * cap, cap)], ql[pl.ds(b * cap, cap)]
            sc[b, :, pl.ds(slot * rows + (t % (rows // width)) * width, width)] = (
                dot_nt(q1, high) + dot_nt(q2, high) + dot_nt(q1, low)
            )
            return carry

        lax.fori_loop(0, 2 * rows // width, step, 0)

    core_landed = remote(slab, pts.at[m_core], core_send.at[0], core_recv.at[0], base + m_core, c)
    core_landed.wait_recv()
    split_points(pts.at[m_core], m_core)
    near_scores(own)

    def arrive(b):
        q_copy(b, ql_send, r, c).wait_recv()

    def round_(s, carry):
        has_left = (s > 0) & (c - s >= 0)
        has_right = (s > 0) & (c + s < C)

        @pl.when(has_left)
        def _():
            b = own - s
            arrive(b)

            @pl.when(c + 1 < C)
            def _():
                q_right(b).start()

            spread(b)

        @pl.when(has_right)
        def _():
            b = own + s
            arrive(b)

            @pl.when(c > 0)
            def _():
                q_left(b).start()

            spread(b)

        @pl.when(has_left)
        def _():
            near_scores(own - s)

        @pl.when(has_right)
        def _():
            near_scores(own + s)

        x_landed(s).wait_recv()
        f_copy(s).start()

        for i in range(1, A):
            other = ((a + i) % A) * C + c

            @pl.when(c - s >= 0)
            def _():
                arrive(other - s)
                near_scores(other - s)

            @pl.when(has_right)
            def _():
                arrive(other + s)
                near_scores(other + s)

        return carry

    lax.fori_loop(0, C, round_, 0)

    def landed(s, carry):
        f_landed(s).wait_recv()
        return carry

    lax.fori_loop(0, C, landed, 0)
    split_points(pts.at[m_x], m_x)
    split_points(pts.at[m_diag], m_diag)

    def far(t, carry):
        slot = 2 * (1 - x) + t // (rows // width)
        part = pl.ds((t % (rows // width)) * width, width)
        out = pl.ds(slot * rows + (t % (rows // width)) * width, width)
        high, low = ph[slot, part], plo[slot, part]
        for b in range(0, NB, 2):
            two = slice(b * cap, (b + 2) * cap)
            value = dot_nt(qh[two], high) + dot_nt(ql[two], high) + dot_nt(qh[two], low)
            sc[b, :, out] = value[0:cap]
            sc[b + 1, :, out] = value[cap:]
        return carry

    lax.fori_loop(0, 2 * rows // width, far, 0)

    slot_id = lax.broadcasted_iota(jnp.int32, (cap, 1), 0).astype(jnp.float32)

    def largest(b, best):
        owner_id = (b % C) * R + (b // C) * QUAD + m
        count = jnp.sum(
            jnp.sum(jnp.where(owner_sel == owner_id, 1.0, 0.0), axis=1, keepdims=True), axis=0, keepdims=True
        )
        value = jnp.where(slot_id < count, sc[b], -1e30)
        return jnp.maximum(best, jnp.max(value, axis=0, keepdims=True))

    mx[m] = lax.fori_loop(0, NB, largest, jnp.full((1, span), -1e30, jnp.float32))

    def m_copy(slot, to):
        return remote(mx.at[slot], mx.at[slot], m_send.at[to], m_recv.at[slot], base + to, c)

    for i in range(1, QUAD):
        m_copy(m, (m + i) % QUAD).start()
    for i in range(1, QUAD):
        m_copy((m + i) % QUAD, (m + i) % QUAD).wait_recv()
    reached = jnp.maximum(jnp.maximum(mx[0], mx[1]), jnp.maximum(mx[2], mx[3]))
    cov[a] = jnp.maximum(cov_old[a], reached)

    def c_copy(slot, to):
        return remote(cov.at[slot], cov.at[slot], c_send.at[to], c_recv.at[slot], to * QUAD + m, c)

    for i in range(1, A):
        c_copy(a, (a + i) % A).start()

    mine = m * NB + own

    def gains(b, carry):
        total = jnp.zeros((cap, 128), jnp.float32)
        for part in range(0, span, 128):
            total = total + jnp.maximum(sc[b, :, part : part + 128] - cov[a, :, part : part + 128], 0.0)
        gr[mine, pl.ds(b, 1)] = jnp.sum(total.T, axis=0, keepdims=True)
        return carry

    lax.fori_loop(0, NB, gains, 0)

    def g_copy(slot, dev):
        return remote(gr.at[slot], gr.at[slot], g_send.at[dev], g_recv.at[slot], dev % R, dev // R)

    def g_start(i, carry):
        g_copy(mine, (me + i) % ND).start()
        return carry

    lax.fori_loop(1, ND, g_start, 0)

    mine_owner = lax.shift_right_logical(cand_col[...], shift)
    rank = jnp.zeros((nk, 1), jnp.float32)
    earlier = lax.broadcasted_iota(jnp.int32, (nk, nk), 1) < lax.broadcasted_iota(jnp.int32, (nk, nk), 0)
    for j in range(R):
        same = jnp.where(owner_sel[j : j + 1] == mine_owner, 1.0, 0.0)
        rank = rank + jnp.sum(same, axis=1, keepdims=True)
        same = jnp.where(owner_cand[j : j + 1] == mine_owner, 1.0, 0.0)
        same = jnp.where((j < r) | ((j == r) & earlier), same, 0.0)
        rank = rank + jnp.sum(same, axis=1, keepdims=True)
    row_of = mine_owner % R
    flat = (row_of % QUAD) * NB + (row_of // QUAD) * C + mine_owner // R
    pick_owner = jnp.where(lax.broadcasted_iota(jnp.int32, (nk, ND), 1) == flat, 1.0, 0.0)
    pick_slot = lax.broadcasted_iota(jnp.int32, (nk, cap), 1).astype(jnp.float32) == rank

    dev_id = lax.broadcasted_iota(jnp.int32, (ND, 1), 0)
    held = jnp.zeros((ND, 1), jnp.float32)
    for j in range(R):
        held = held + jnp.sum(jnp.where(owner_sel[j : j + 1] == dev_id, 1.0, 0.0), axis=1, keepdims=True)
        held = held + jnp.sum(jnp.where(owner_cand[j : j + 1] == dev_id, 1.0, 0.0), axis=1, keepdims=True)
    flag_out[...] = jnp.broadcast_to(jnp.max(held, axis=0, keepdims=True), flag_out.shape)

    for i in range(1, A):
        c_copy((a + i) % A, (a + i) % A).wait_recv()
    cov_out[...] = cov[...]

    def g_wait(i, carry):
        dev = (me + i) % ND
        row, col = dev % R, dev // R
        g_copy((row % QUAD) * NB + (row // QUAD) * C + col, dev).wait_recv()
        return carry

    lax.fori_loop(1, ND, g_wait, 0)
    totals = jnp.concatenate(
        [jnp.sum(gr[i * NB : (i + 1) * NB], axis=0) for i in range(QUAD)], axis=0
    )
    spread_gain = jnp.dot(pick_owner, totals, precision=lax.Precision.HIGHEST, preferred_element_type=jnp.float32)
    gain_out[...] = jnp.sum(jnp.where(pick_slot, spread_gain, 0.0), axis=1, keepdims=True)

    for i in range(1, R):
        idx_copy(r, (r + i) % R).wait_send()
    core_copy.wait_send()

    def left(s, carry):
        x_copy(s).wait_send()
        f_copy(s).wait_send()

        @pl.when(c - s >= 0)
        def _():
            @pl.when(c + 1 < C)
            def _():
                q_right(own - s).wait_send()

            for i in range(1, A):
                q_across(own - s, i).wait_send()

        @pl.when(c + s < C)
        def _():
            @pl.when(c > 0)
            def _():
                q_left(own + s).wait_send()

            @pl.when(s > 0)
            def _():
                for i in range(1, A):
                    q_across(own + s, i).wait_send()

        return carry

    lax.fori_loop(0, C, left, 0)
    for i in range(1, QUAD):
        m_copy(m, (m + i) % QUAD).wait_send()
    for i in range(1, A):
        c_copy(a, (a + i) % A).wait_send()

    def g_left(i, carry):
        g_copy(mine, (me + i) % ND).wait_send()
        return carry

    lax.fori_loop(1, ND, g_left, 0)


def fused(R, C, slab_embed, coverage_old, sel_index, cand_index):
    rows, depth = slab_embed.shape
    ns, nk = sel_index.shape[0], cand_index.shape[0]
    A, ND = R // QUAD, R * C
    NB = A * C
    span = QUAD * rows
    mean = (ns + nk) * R / ND
    cap = int(-(-mean * 1.5 // 32)) * 32
    width = -(-(ns + nk) // 128) * 128
    f32, bf16, dma = jnp.float32, jnp.bfloat16, pltpu.SemaphoreType.DMA
    vmem = pl.BlockSpec(memory_space=pltpu.VMEM)
    coverage, gain, held = pl.pallas_call(
        functools.partial(kernel, R, C, cap),
        out_shape=(
            jax.ShapeDtypeStruct((A, 1, span), f32),
            jax.ShapeDtypeStruct((nk, 1), f32),
            jax.ShapeDtypeStruct((8, 128), f32),
        ),
        in_specs=[vmem] * 5,
        out_specs=(vmem, vmem, vmem),
        scratch_shapes=[
            pltpu.VMEM((QUAD, rows, depth), f32),
            pltpu.VMEM((QUAD, rows, depth), bf16),
            pltpu.VMEM((QUAD, rows, depth), bf16),
            pltpu.VMEM((NB, cap, depth), f32),
            pltpu.VMEM((NB * cap, depth), bf16),
            pltpu.VMEM((NB * cap, depth), bf16),
            pltpu.VMEM((NB, cap, span), f32),
            pltpu.VMEM((R, 1, width), jnp.int32),
            pltpu.VMEM((QUAD, 1, span), f32),
            pltpu.VMEM((A, 1, span), f32),
            pltpu.VMEM((8, 128), f32),
            pltpu.VMEM((ND, NB, cap), f32),
            dma((R,)), dma((R,)), dma((1,)), dma((1,)), dma((C,)), dma((C,)), dma((C,)), dma((C,)),
            dma((NB,)), dma((NB,)), dma((NB,)), dma((A - 1, NB)),
            dma((QUAD,)), dma((QUAD,)), dma((A,)), dma((A,)), dma((ND,)), dma((ND,)),
        ],
        compiler_params=pltpu.CompilerParams(
            collective_id=0, has_side_effects=True, vmem_limit_bytes=58 * 1024 * 1024
        ),
        cost_estimate=pl.CostEstimate(
            flops=6 * NB * cap * span * depth, bytes_accessed=rows * depth * 4, transcendentals=0
        ),
    )(
        slab_embed,
        coverage_old.reshape(A, 1, span),
        sel_index.reshape(1, ns),
        cand_index.reshape(1, nk),
        cand_index.reshape(nk, 1),
    )
    return coverage.reshape(A * span), gain.reshape(nk), held[0, 0] > cap


def body(R, C, slab_embed, coverage_old, sel_index, cand_index):
    coverage, gain, crowded = fused(R, C, slab_embed, coverage_old, sel_index, cand_index)
    return lax.cond(
        crowded,
        lambda: any_draw(slab_embed, coverage_old, sel_index, cand_index),
        lambda: (coverage, gain),
    )


def solution(mesh):
    in_specs = (P(("col", "row"), None), P("col"), P("row"), P("row"))
    out_specs = (P("col"), P("row"))
    return jax.shard_map(
        functools.partial(body, mesh.shape["row"], mesh.shape["col"]),
        mesh=mesh, in_specs=in_specs, out_specs=out_specs, check_vma=False,
    )
```

```python
import functools

import jax
import jax.numpy as jnp
from jax import lax
from jax.experimental import pallas as pl
from jax.experimental.pallas import tpu as pltpu
from jax.sharding import PartitionSpec as P

MESH = pl.DeviceIdType.MESH
QUAD = 4
NT = (((1,), (1,)), ((), ()))


def similar(left, right):
    return lax.dot_general(
        left,
        right,
        (((1,), (1,)), ((), ())),
        precision=lax.Precision.HIGHEST,
        preferred_element_type=jnp.float32,
    )


def lookup(source, indices, first_row):
    position = indices - first_row
    inside = (position >= 0) & (position < source.shape[0])
    picked = jnp.take(source, jnp.clip(position, 0, source.shape[0] - 1), axis=0)
    return jnp.where(inside[:, None], picked, 0.0)


def any_draw(slab_embed, coverage_old, sel_index, cand_index):
    col_id = lax.axis_index("col")
    gathered = lax.all_gather(slab_embed, "row", axis=0, tiled=True)
    first_row = col_id * gathered.shape[0]
    selected, chosen = lax.psum(
        (lookup(gathered, sel_index, first_row), lookup(gathered, cand_index, first_row)), "col"
    )
    partial_value = jnp.max(similar(selected, gathered), axis=0)
    reached = lax.pmax(partial_value, "row")
    coverage = jnp.maximum(coverage_old, reached)
    gain_part = jnp.sum(jnp.maximum(similar(chosen, gathered) - coverage[None, :], 0.0), axis=1)
    return coverage, lax.psum(gain_part, "col")


def halves(value):
    high = value.astype(jnp.bfloat16)
    return high, (value - high.astype(jnp.float32)).astype(jnp.bfloat16)


def dot_nt(left, right):
    return lax.dot_general(left, right, NT, preferred_element_type=jnp.float32)


def kernel(
    R, C, cap, slab, cov_old, sel, cand,
    cov_out, gain_out, flag_out,
    pts, ph, plo, qs, qh, ql, sc, idx, bias, best, mx, cov, gr,
    idx_send, idx_recv, core_send, core_recv, x_send, x_recv, f_send, f_recv,
    q_recv, ql_send, qr_send, qa_send, m_send, m_recv, c_send, c_recv, g_send, g_recv,
):
    A = R // QUAD
    NB = A * C
    ND = R * C
    rows = slab.shape[0]
    ns, nk = sel.shape[1], cand.shape[1]
    shift = rows.bit_length() - 1
    span = QUAD * rows
    r = lax.axis_index("row")
    c = lax.axis_index("col")
    me = c * R + r
    a = lax.div(r, QUAD)
    m = lax.rem(r, QUAD)
    x, h = lax.div(m, 2), lax.rem(m, 2)
    m_core = 2 * x + (1 - h)
    m_x = 2 * (1 - x) + h
    m_diag = 2 * (1 - x) + (1 - h)
    base = a * QUAD
    width = 256
    parts = rows // width

    def remote(src, dst, ssem, rsem, row, col):
        return pltpu.make_async_remote_copy(
            src_ref=src, dst_ref=dst, send_sem=ssem, recv_sem=rsem,
            device_id=(row, col), device_id_type=MESH,
        )

    barrier = pltpu.get_barrier_semaphore()

    def greet(i, carry):
        dev = lax.rem(me + i, ND)
        pl.semaphore_signal(barrier, inc=1, device_id=(lax.rem(dev, R), lax.div(dev, R)), device_id_type=MESH)
        return carry

    lax.fori_loop(1, ND, greet, 0)
    idx[r] = jnp.full(idx.shape[1:], -1, jnp.int32)
    idx[r, :, 0:ns] = sel[...]
    idx[r, :, ns : ns + nk] = cand[...]
    pl.semaphore_wait(barrier, ND - 1)

    def idx_copy(slot, to):
        return remote(idx.at[slot], idx.at[slot], idx_send.at[to], idx_recv.at[slot], to, c)

    for i in range(1, R):
        idx_copy(r, lax.rem(r + i, R)).start()

    core_copy = remote(slab, pts.at[m], core_send.at[0], core_recv.at[0], base + m_core, c)
    core_copy.start()

    def x_copy(s):
        part = pl.ds(s * width, width)
        return remote(slab.at[part], pts.at[m, part], x_send.at[s], x_recv.at[s], base + m_x, c)

    def x_landed(s):
        part = pl.ds(s * width, width)
        return remote(slab.at[part], pts.at[m_x, part], x_send.at[s], x_recv.at[s], base + m_x, c)

    def f_copy(s):
        part = pl.ds(s * width, width)
        return remote(pts.at[m_x, part], pts.at[m_x, part], f_send.at[s], f_recv.at[s], base + m_core, c)

    def f_landed(s):
        part = pl.ds(s * width, width)
        return remote(pts.at[m_diag, part], pts.at[m_diag, part], f_send.at[s], f_recv.at[s], base + m_core, c)

    for s in range(parts):
        x_copy(s).start()

    def split_part(source, slot, s):
        part = pl.ds(s * width, width)
        high, low = halves(source[part])
        ph[slot, part] = high
        plo[slot, part] = low

    def split_points(source, slot):
        for s in range(parts):
            split_part(source, slot, s)

    best[...] = jnp.full(best.shape, -1e30, jnp.float32)
    split_points(slab, m)

    for i in range(1, R):
        idx_copy(lax.rem(r + i, R), lax.rem(r + i, R)).wait_recv()

    everything = jnp.concatenate([idx[j] for j in range(R)], axis=0)
    owner = lax.shift_right_logical(everything, shift)
    local = (everything - owner * rows).astype(jnp.float32)
    owner_sel, owner_cand = owner[:, 0:ns], owner[:, ns:]
    slot_id = lax.broadcasted_iota(jnp.int32, (cap, 128), 0).astype(jnp.float32)

    def place(owners, locals_, start, packed):
        n = owners.shape[1]
        mask = jnp.where(owners == me, 1.0, 0.0)
        before = lax.broadcasted_iota(jnp.int32, (n, n), 0) < lax.broadcasted_iota(jnp.int32, (n, n), 1)
        within = jnp.dot(
            mask.astype(jnp.bfloat16), before.astype(jnp.bfloat16), preferred_element_type=jnp.float32
        )
        for j in range(R):
            rank = jnp.where(mask[j : j + 1] > 0.0, within[j : j + 1] + start, -1.0)
            spot = locals_[j : j + 1] + 1.0
            for lane in range(0, n, 128):
                packed = packed + jnp.where(
                    rank[:, lane : lane + 128] == slot_id, spot[:, lane : lane + 128], 0.0
                )
            start = start + jnp.sum(mask[j : j + 1], axis=1, keepdims=True)
        return start, packed

    start, packed = place(
        owner_sel, local[:, 0:ns], jnp.zeros((1, 1), jnp.float32), jnp.zeros((cap, 128), jnp.float32)
    )
    start, packed = place(owner_cand, local[:, ns:], start, packed)
    packed = jnp.sum(packed, axis=1, keepdims=True)
    point = lax.broadcasted_iota(jnp.int32, (cap, rows), 1).astype(jnp.float32)
    pick = jnp.where(point == packed - 1.0, 1.0, 0.0)
    own = a * C + c
    qs[own] = jnp.dot(pick, slab[...], precision=lax.Precision.HIGHEST, preferred_element_type=jnp.float32)

    def q_copy(b, ssem, row, col):
        return remote(qs.at[b], qs.at[b], ssem.at[b], q_recv.at[b], row, col)

    def q_right(b):
        return q_copy(b, qr_send, r, c + 1)

    def q_left(b):
        return q_copy(b, ql_send, r, c - 1)

    def q_across(b, i):
        return q_copy(b, qa_send.at[i - 1], (lax.rem(a + i, A)) * QUAD + m, c)

    def spread(b):
        for i in range(1, A):
            q_across(b, i).start()

    @pl.when(c + 1 < C)
    def _():
        q_right(own).start()

    @pl.when(c > 0)
    def _():
        q_left(own).start()

    spread(own)

    def split_block(b):
        high, low = halves(qs[b])
        qh[pl.ds(b * cap, cap)] = high
        ql[pl.ds(b * cap, cap)] = low

    def score(first, count, slot, s):
        part = pl.ds(s * width, width)
        out = pl.ds(slot * rows + s * width, width)
        block = pl.ds(first * cap, count * cap)
        high, low = ph[slot, part], plo[slot, part]
        value = dot_nt(qh[block], high) + dot_nt(ql[block], high) + dot_nt(qh[block], low)
        sc[block, out] = value
        shift_by = bias[block]
        top = jnp.concatenate(
            [
                jnp.max(
                    (value[:, lane : lane + 128] + shift_by).reshape(count * cap // 8, 8, 128), axis=0
                )
                for lane in range(0, width, 128)
            ],
            axis=1,
        )
        best[:, out] = jnp.maximum(best[:, out], top)

    def near_scores(b):
        split_block(b)

        def step(t, carry):
            score(b, 1, 2 * x + lax.div(t, parts), lax.rem(t, parts))
            return carry

        lax.fori_loop(0, 2 * parts, step, 0)

    core_landed = remote(slab, pts.at[m_core], core_send.at[0], core_recv.at[0], base + m_core, c)
    core_landed.wait_recv()
    split_points(pts.at[m_core], m_core)
    def mark(b, carry):
        owner_id = lax.rem(b, C) * R + lax.div(b, C) * QUAD + m
        count = jnp.sum(
            jnp.sum(jnp.where(owner_sel == owner_id, 1.0, 0.0), axis=1, keepdims=True), axis=0, keepdims=True
        )
        bias[pl.ds(b * cap, cap)] = jnp.where(slot_id < count, 0.0, -1e30)
        return carry

    lax.fori_loop(0, NB, mark, 0)
    near_scores(own)

    square = (nk, nk)
    across, down = lax.broadcasted_iota(jnp.int32, square, 1), lax.broadcasted_iota(jnp.int32, square, 0)
    mine_row = lax.shift_right_logical(cand[...], shift).astype(jnp.float32)
    mine_owner = jnp.sum(jnp.where(across == down, mine_row, 0.0), axis=1, keepdims=True).astype(jnp.int32)
    wide = owner_cand.shape[1]
    earlier = lax.broadcasted_iota(jnp.int32, (nk, wide), 1) < lax.broadcasted_iota(jnp.int32, (nk, wide), 0)
    same_total = jnp.zeros((nk, 128), jnp.float32)
    for j in range(R):
        same = jnp.where(owner_sel[j : j + 1] == mine_owner, 1.0, 0.0)
        for lane in range(0, ns, 128):
            same_total = same_total + same[:, lane : lane + 128]
        counted = (j < r) | ((j == r) & earlier)
        same = jnp.where(counted & (owner_cand[j : j + 1] == mine_owner), 1.0, 0.0)
        for lane in range(0, wide, 128):
            same_total = same_total + same[:, lane : lane + 128]
    rank = jnp.sum(same_total, axis=1, keepdims=True)
    row_of = lax.rem(mine_owner, R)
    flat = lax.rem(row_of, QUAD) * NB + lax.div(row_of, QUAD) * C + lax.div(mine_owner, R)
    pick_owner = jnp.where(lax.broadcasted_iota(jnp.int32, (nk, ND), 1) == flat, 1.0, 0.0)
    pick_slot = lax.broadcasted_iota(jnp.int32, (nk, cap), 1).astype(jnp.float32) == rank

    dev_id = lax.broadcasted_iota(jnp.int32, (ND, 1), 0)
    held = jnp.zeros((ND, 128), jnp.float32)
    for j in range(R):
        for lane in range(0, ns + wide, 128):
            held = held + jnp.where(owner[j : j + 1, lane : lane + 128] == dev_id, 1.0, 0.0)
    held = jnp.sum(held, axis=1, keepdims=True)
    flag_out[...] = jnp.max(held, axis=0, keepdims=True)

    def arrive(b):
        q_copy(b, ql_send, r, c).wait_recv()

    def across_blocks(s):
        for i in range(1, A):
            other = lax.rem(a + i, A) * C + c

            @pl.when(c - s >= 0)
            def _():
                arrive(other - s)
                near_scores(other - s)

            @pl.when((s > 0) & (c + s < C))
            def _():
                arrive(other + s)
                near_scores(other + s)

    def round_(s, carry):
        has_left = (s < C) & (c - s >= 0)
        has_right = (s < C) & (c + s < C)

        @pl.when(has_left)
        def _():
            b = own - s
            arrive(b)

            @pl.when(c + 1 < C)
            def _():
                q_right(b).start()

            spread(b)

        @pl.when(has_right)
        def _():
            b = own + s
            arrive(b)

            @pl.when(c > 0)
            def _():
                q_left(b).start()

            spread(b)

        @pl.when(has_left)
        def _():
            near_scores(own - s)

        @pl.when(has_right)
        def _():
            near_scores(own + s)

        @pl.when(s == C)
        def _():
            for t in range(parts):
                x_landed(t).wait_recv()
                f_copy(t).start()

            def step(t, carry):
                split_part(pts.at[m_x], m_x, t)
                score(a * C, C, m_x, t)
                return carry

            lax.fori_loop(0, parts, step, 0)

        across_blocks(s - 1)
        return carry

    lax.fori_loop(1, C + 1, round_, 0)
    for t in range(parts):
        f_landed(t).wait_recv()
        split_part(pts.at[m_diag], m_diag, t)

    def far(t, carry):
        score(a * C, C, m_diag, t)
        return carry

    lax.fori_loop(0, parts, far, 0)
    for i in range(1, A):
        other = lax.rem(a + i, A) * C

        def far_across(t, carry):
            score(other, C, 2 * (1 - x) + lax.div(t, parts), lax.rem(t, parts))
            return carry

        lax.fori_loop(0, 2 * parts, far_across, 0)

    mx[m] = jnp.max(best[...], axis=0, keepdims=True)

    def m_copy(slot, to):
        return remote(mx.at[slot], mx.at[slot], m_send.at[to], m_recv.at[slot], base + to, c)

    for i in range(1, QUAD):
        m_copy(m, lax.rem(m + i, QUAD)).start()
    for i in range(1, QUAD):
        m_copy(lax.rem(m + i, QUAD), lax.rem(m + i, QUAD)).wait_recv()
    reached = jnp.maximum(jnp.maximum(mx[0], mx[1]), jnp.maximum(mx[2], mx[3]))
    cov[a] = jnp.maximum(cov_old[a], reached)

    def c_copy(slot, to):
        return remote(cov.at[slot], cov.at[slot], c_send.at[to], c_recv.at[slot], to * QUAD + m, c)

    for i in range(1, A):
        c_copy(a, lax.rem(a + i, A)).start()

    mine = m * NB + own

    def gains(b, carry):
        total = jnp.zeros((cap, 128), jnp.float32)
        for part in range(0, span, 128):
            total = total + jnp.maximum(sc[pl.ds(b * cap, cap), part : part + 128] - cov[a, :, part : part + 128], 0.0)
        gr[mine, pl.ds(b, 1)] = jnp.sum(total.T, axis=0, keepdims=True)
        return carry

    lax.fori_loop(0, NB, gains, 0)

    def g_copy(slot, dev):
        return remote(
            gr.at[slot], gr.at[slot], g_send.at[dev], g_recv.at[slot], lax.rem(dev, R), lax.div(dev, R)
        )

    def g_start(i, carry):
        g_copy(mine, lax.rem(me + i, ND)).start()
        return carry

    lax.fori_loop(1, ND, g_start, 0)

    for i in range(1, A):
        c_copy(lax.rem(a + i, A), lax.rem(a + i, A)).wait_recv()
    cov_out[...] = cov[...]

    def g_wait(i, carry):
        dev = lax.rem(me + i, ND)
        row, col = lax.rem(dev, R), lax.div(dev, R)
        g_copy(lax.rem(row, QUAD) * NB + lax.div(row, QUAD) * C + col, dev).wait_recv()
        return carry

    lax.fori_loop(1, ND, g_wait, 0)
    totals = jnp.concatenate(
        [jnp.sum(gr[i * NB : (i + 1) * NB], axis=0) for i in range(QUAD)], axis=0
    )
    spread_gain = jnp.dot(pick_owner, totals, precision=lax.Precision.HIGHEST, preferred_element_type=jnp.float32)
    gain_out[...] = jnp.sum(jnp.where(pick_slot, spread_gain, 0.0), axis=1, keepdims=True)

    for i in range(1, R):
        idx_copy(r, lax.rem(r + i, R)).wait_send()
    core_copy.wait_send()

    for s in range(parts):
        x_copy(s).wait_send()
        f_copy(s).wait_send()

    def left(s, carry):
        @pl.when(c - s >= 0)
        def _():
            @pl.when(c + 1 < C)
            def _():
                q_right(own - s).wait_send()

            for i in range(1, A):
                q_across(own - s, i).wait_send()

        @pl.when(c + s < C)
        def _():
            @pl.when(c > 0)
            def _():
                q_left(own + s).wait_send()

            @pl.when(s > 0)
            def _():
                for i in range(1, A):
                    q_across(own + s, i).wait_send()

        return carry

    lax.fori_loop(0, C, left, 0)
    for i in range(1, QUAD):
        m_copy(m, lax.rem(m + i, QUAD)).wait_send()
    for i in range(1, A):
        c_copy(a, lax.rem(a + i, A)).wait_send()

    def g_left(i, carry):
        g_copy(mine, lax.rem(me + i, ND)).wait_send()
        return carry

    lax.fori_loop(1, ND, g_left, 0)


def fused(R, C, slab_embed, coverage_old, sel_index, cand_index):
    rows, depth = slab_embed.shape
    ns, nk = sel_index.shape[0], cand_index.shape[0]
    A, ND = R // QUAD, R * C
    NB = A * C
    span = QUAD * rows
    mean = (ns + nk) * R / ND
    cap = int(-(-mean * 1.5 // 32)) * 32
    width = -(-(ns + nk) // 128) * 128
    parts = rows // 256
    f32, bf16, dma = jnp.float32, jnp.bfloat16, pltpu.SemaphoreType.DMA
    vmem = pl.BlockSpec(memory_space=pltpu.VMEM)
    coverage, gain, held = pl.pallas_call(
        functools.partial(kernel, R, C, cap),
        out_shape=(
            jax.ShapeDtypeStruct((A, 1, span), f32),
            jax.ShapeDtypeStruct((nk, 1), f32),
            jax.ShapeDtypeStruct((1, 1), f32),
        ),
        in_specs=[vmem] * 4,
        out_specs=(vmem, vmem, vmem),
        scratch_shapes=[
            pltpu.VMEM((QUAD, rows, depth), f32),
            pltpu.VMEM((QUAD, rows, depth), bf16),
            pltpu.VMEM((QUAD, rows, depth), bf16),
            pltpu.VMEM((NB, cap, depth), f32),
            pltpu.VMEM((NB * cap, depth), bf16),
            pltpu.VMEM((NB * cap, depth), bf16),
            pltpu.VMEM((NB * cap, span), f32),
            pltpu.VMEM((R, 1, width), jnp.int32),
            pltpu.VMEM((NB * cap, 128), f32),
            pltpu.VMEM((8, span), f32),
            pltpu.VMEM((QUAD, 1, span), f32),
            pltpu.VMEM((A, 1, span), f32),
            pltpu.VMEM((ND, NB, cap), f32),
            dma((R,)), dma((R,)), dma((1,)), dma((1,)),
            dma((parts,)), dma((parts,)), dma((parts,)), dma((parts,)),
            dma((NB,)), dma((NB,)), dma((NB,)), dma((A - 1, NB)),
            dma((QUAD,)), dma((QUAD,)), dma((A,)), dma((A,)), dma((ND,)), dma((ND,)),
        ],
        compiler_params=pltpu.CompilerParams(
            collective_id=0, has_side_effects=True, vmem_limit_bytes=58 * 1024 * 1024
        ),
        cost_estimate=pl.CostEstimate(
            flops=6 * NB * cap * span * depth, bytes_accessed=rows * depth * 4, transcendentals=0
        ),
    )(
        slab_embed,
        coverage_old.reshape(A, 1, span),
        sel_index.reshape(1, ns),
        cand_index.reshape(1, nk),
    )
    return coverage.reshape(A * span), gain.reshape(nk), held[0, 0] > cap


def body(R, C, slab_embed, coverage_old, sel_index, cand_index):
    coverage, gain, crowded = fused(R, C, slab_embed, coverage_old, sel_index, cand_index)
    return lax.cond(
        crowded,
        lambda: any_draw(slab_embed, coverage_old, sel_index, cand_index),
        lambda: (coverage, gain),
    )


def solution(mesh):
    in_specs = (P(("col", "row"), None), P("col"), P("row"), P("row"))
    out_specs = (P("col"), P("row"))
    return jax.shard_map(
        functools.partial(body, mesh.shape["row"], mesh.shape["col"]),
        mesh=mesh, in_specs=in_specs, out_specs=out_specs, check_vma=False,
    )
```

```python
import functools

import jax
import jax.numpy as jnp
from jax import lax
from jax.experimental import pallas as pl
from jax.experimental.pallas import tpu as pltpu
from jax.sharding import PartitionSpec as P

MESH = pl.DeviceIdType.MESH
QUAD = 4
NT = (((1,), (1,)), ((), ()))


def similar(left, right):
    return lax.dot_general(
        left,
        right,
        (((1,), (1,)), ((), ())),
        precision=lax.Precision.HIGHEST,
        preferred_element_type=jnp.float32,
    )


def lookup(source, indices, first_row):
    position = indices - first_row
    inside = (position >= 0) & (position < source.shape[0])
    picked = jnp.take(source, jnp.clip(position, 0, source.shape[0] - 1), axis=0)
    return jnp.where(inside[:, None], picked, 0.0)


def any_draw(slab_embed, coverage_old, sel_index, cand_index):
    col_id = lax.axis_index("col")
    gathered = lax.all_gather(slab_embed, "row", axis=0, tiled=True)
    first_row = col_id * gathered.shape[0]
    selected, chosen = lax.psum(
        (lookup(gathered, sel_index, first_row), lookup(gathered, cand_index, first_row)), "col"
    )
    partial_value = jnp.max(similar(selected, gathered), axis=0)
    reached = lax.pmax(partial_value, "row")
    coverage = jnp.maximum(coverage_old, reached)
    gain_part = jnp.sum(jnp.maximum(similar(chosen, gathered) - coverage[None, :], 0.0), axis=1)
    return coverage, lax.psum(gain_part, "col")


def halves(value):
    high = value.astype(jnp.bfloat16)
    return high, (value - high.astype(jnp.float32)).astype(jnp.bfloat16)


def dot_nt(left, right):
    return lax.dot_general(left, right, NT, preferred_element_type=jnp.float32)


def kernel(
    R, C, cap, sent, slab, cov_old, sel, cand,
    cov_out, gain_out, flag_out,
    pts, ph, plo, qs, qh, ql, sc, idx, bias, best, mx, cov, gr,
    idx_send, idx_recv, core_send, core_recv, x_send, x_recv, f_send, f_recv,
    q_recv, ql_send, qr_send, qa_send, m_send, m_recv, c_send, c_recv, g_send, g_recv,
):
    A = R // QUAD
    NB = A * C
    ND = R * C
    rows = slab.shape[0]
    ns, nk = sel.shape[1], cand.shape[1]
    shift = rows.bit_length() - 1
    span = QUAD * rows
    r = lax.axis_index("row")
    c = lax.axis_index("col")
    me = c * R + r
    a = lax.div(r, QUAD)
    m = lax.rem(r, QUAD)
    x, h = lax.div(m, 2), lax.rem(m, 2)
    m_core = 2 * x + (1 - h)
    m_x = 2 * (1 - x) + h
    m_diag = 2 * (1 - x) + (1 - h)
    base = a * QUAD
    width = 256
    parts = rows // width

    def remote(src, dst, ssem, rsem, row, col):
        return pltpu.make_async_remote_copy(
            src_ref=src, dst_ref=dst, send_sem=ssem, recv_sem=rsem,
            device_id=(row, col), device_id_type=MESH,
        )

    barrier = pltpu.get_barrier_semaphore()

    def greet(i, carry):
        dev = lax.rem(me + i, ND)
        pl.semaphore_signal(barrier, inc=1, device_id=(lax.rem(dev, R), lax.div(dev, R)), device_id_type=MESH)
        return carry

    lax.fori_loop(1, ND, greet, 0)
    idx[r] = jnp.full(idx.shape[1:], -1, jnp.int32)
    idx[r, :, 0:ns] = sel[...]
    idx[r, :, ns : ns + nk] = cand[...]
    pl.semaphore_wait(barrier, ND - 1)

    def idx_copy(slot, to):
        return remote(idx.at[slot], idx.at[slot], idx_send.at[to], idx_recv.at[slot], to, c)

    for i in range(1, R):
        idx_copy(r, lax.rem(r + i, R)).start()

    core_copy = remote(slab, pts.at[m], core_send.at[0], core_recv.at[0], base + m_core, c)
    core_copy.start()

    def x_copy(s):
        part = pl.ds(s * width, width)
        return remote(slab.at[part], pts.at[m, part], x_send.at[s], x_recv.at[s], base + m_x, c)

    def x_landed(s):
        part = pl.ds(s * width, width)
        return remote(slab.at[part], pts.at[m_x, part], x_send.at[s], x_recv.at[s], base + m_x, c)

    def f_copy(s):
        part = pl.ds(s * width, width)
        return remote(pts.at[m_x, part], pts.at[m_x, part], f_send.at[s], f_recv.at[s], base + m_core, c)

    def f_landed(s):
        part = pl.ds(s * width, width)
        return remote(pts.at[m_diag, part], pts.at[m_diag, part], f_send.at[s], f_recv.at[s], base + m_core, c)

    for s in range(parts):
        x_copy(s).start()

    def split_part(source, slot, s):
        part = pl.ds(s * width, width)
        high, low = halves(source[part])
        ph[slot, part] = high
        plo[slot, part] = low

    def split_points(source, slot):
        for s in range(parts):
            split_part(source, slot, s)

    if sent < cap:
        qs[:, sent:] = jnp.zeros((NB, cap - sent, qs.shape[2]), jnp.float32)
    best[...] = jnp.full(best.shape, -1e30, jnp.float32)
    split_points(slab, m)

    for i in range(1, R):
        idx_copy(lax.rem(r + i, R), lax.rem(r + i, R)).wait_recv()

    everything = jnp.concatenate([idx[j] for j in range(R)], axis=0)
    owner = lax.shift_right_logical(everything, shift)
    local = (everything - owner * rows).astype(jnp.float32)
    owner_sel, owner_cand = owner[:, 0:ns], owner[:, ns:]
    slot_id = lax.broadcasted_iota(jnp.int32, (cap, 128), 0).astype(jnp.float32)

    def place(owners, locals_, start, packed):
        n = owners.shape[1]
        mask = jnp.where(owners == me, 1.0, 0.0)
        before = lax.broadcasted_iota(jnp.int32, (n, n), 0) < lax.broadcasted_iota(jnp.int32, (n, n), 1)
        within = jnp.dot(
            mask.astype(jnp.bfloat16), before.astype(jnp.bfloat16), preferred_element_type=jnp.float32
        )
        for j in range(R):
            rank = jnp.where(mask[j : j + 1] > 0.0, within[j : j + 1] + start, -1.0)
            spot = locals_[j : j + 1] + 1.0
            for lane in range(0, n, 128):
                packed = packed + jnp.where(
                    rank[:, lane : lane + 128] == slot_id, spot[:, lane : lane + 128], 0.0
                )
            start = start + jnp.sum(mask[j : j + 1], axis=1, keepdims=True)
        return start, packed

    start, packed = place(
        owner_sel, local[:, 0:ns], jnp.zeros((1, 1), jnp.float32), jnp.zeros((cap, 128), jnp.float32)
    )
    start, packed = place(owner_cand, local[:, ns:], start, packed)
    packed = jnp.sum(packed, axis=1, keepdims=True)
    point = lax.broadcasted_iota(jnp.int32, (cap, rows), 1).astype(jnp.float32)
    pick = jnp.where(point == packed - 1.0, 1.0, 0.0)
    own = a * C + c
    rows_owned = jnp.dot(pick, slab[...], precision=lax.Precision.HIGHEST, preferred_element_type=jnp.float32)
    qs[own, 0:sent] = rows_owned[0:sent]

    def q_copy(b, ssem, row, col):
        part = qs.at[b, pl.ds(0, sent)]
        return remote(part, part, ssem.at[b], q_recv.at[b], row, col)

    def q_right(b):
        return q_copy(b, qr_send, r, c + 1)

    def q_left(b):
        return q_copy(b, ql_send, r, c - 1)

    def q_across(b, i):
        return q_copy(b, qa_send.at[i - 1], (lax.rem(a + i, A)) * QUAD + m, c)

    def spread(b):
        for i in range(1, A):
            q_across(b, i).start()

    @pl.when(c + 1 < C)
    def _():
        q_right(own).start()

    @pl.when(c > 0)
    def _():
        q_left(own).start()

    spread(own)

    def split_block(b):
        high, low = halves(qs[b])
        qh[pl.ds(b * cap, cap)] = high
        ql[pl.ds(b * cap, cap)] = low

    def score(first, count, slot, s):
        part = pl.ds(s * width, width)
        out = pl.ds(slot * rows + s * width, width)
        block = pl.ds(first * cap, count * cap)
        high, low = ph[slot, part], plo[slot, part]
        n = count * cap
        both = dot_nt(jnp.concatenate([qh[block], ql[block]], axis=0), high)
        value = both[0:n] + both[n:] + dot_nt(qh[block], low)
        sc[block, out] = value
        shift_by = bias[block]
        top = jnp.concatenate(
            [
                jnp.max(
                    (value[:, lane : lane + 128] + shift_by).reshape(n // 8, 8, 128), axis=0
                )
                for lane in range(0, width, 128)
            ],
            axis=1,
        )
        best[:, out] = jnp.maximum(best[:, out], top)

    def near_scores(b):
        split_block(b)

        def step(t, carry):
            score(b, 1, 2 * x + lax.div(t, parts), lax.rem(t, parts))
            return carry

        lax.fori_loop(0, 2 * parts, step, 0)

    core_landed = remote(slab, pts.at[m_core], core_send.at[0], core_recv.at[0], base + m_core, c)
    core_landed.wait_recv()
    split_points(pts.at[m_core], m_core)
    def mark(b, carry):
        owner_id = lax.rem(b, C) * R + lax.div(b, C) * QUAD + m
        count = jnp.sum(
            jnp.sum(jnp.where(owner_sel == owner_id, 1.0, 0.0), axis=1, keepdims=True), axis=0, keepdims=True
        )
        bias[pl.ds(b * cap, cap)] = jnp.where(slot_id < count, 0.0, -1e30)
        return carry

    lax.fori_loop(0, NB, mark, 0)
    near_scores(own)

    square = (nk, nk)
    across, down = lax.broadcasted_iota(jnp.int32, square, 1), lax.broadcasted_iota(jnp.int32, square, 0)
    mine_row = lax.shift_right_logical(cand[...], shift).astype(jnp.float32)
    mine_owner = jnp.sum(jnp.where(across == down, mine_row, 0.0), axis=1, keepdims=True).astype(jnp.int32)
    wide = owner_cand.shape[1]
    earlier = lax.broadcasted_iota(jnp.int32, (nk, wide), 1) < lax.broadcasted_iota(jnp.int32, (nk, wide), 0)
    same_total = jnp.zeros((nk, 128), jnp.float32)
    for j in range(R):
        same = jnp.where(owner_sel[j : j + 1] == mine_owner, 1.0, 0.0)
        for lane in range(0, ns, 128):
            same_total = same_total + same[:, lane : lane + 128]
        counted = (j < r) | ((j == r) & earlier)
        same = jnp.where(counted & (owner_cand[j : j + 1] == mine_owner), 1.0, 0.0)
        for lane in range(0, wide, 128):
            same_total = same_total + same[:, lane : lane + 128]
    rank = jnp.sum(same_total, axis=1, keepdims=True)
    row_of = lax.rem(mine_owner, R)
    flat = lax.rem(row_of, QUAD) * NB + lax.div(row_of, QUAD) * C + lax.div(mine_owner, R)
    pick_owner = jnp.where(lax.broadcasted_iota(jnp.int32, (nk, ND), 1) == flat, 1.0, 0.0)
    pick_slot = lax.broadcasted_iota(jnp.int32, (nk, cap), 1).astype(jnp.float32) == rank

    dev_id = lax.broadcasted_iota(jnp.int32, (ND, 1), 0)
    held = jnp.zeros((ND, 128), jnp.float32)
    for j in range(R):
        for lane in range(0, ns + wide, 128):
            held = held + jnp.where(owner[j : j + 1, lane : lane + 128] == dev_id, 1.0, 0.0)
    held = jnp.sum(held, axis=1, keepdims=True)
    flag_out[...] = jnp.max(held, axis=0, keepdims=True)

    def arrive(b):
        q_copy(b, ql_send, r, c).wait_recv()

    def across_blocks(s):
        for i in range(1, A):
            other = lax.rem(a + i, A) * C + c

            @pl.when(c - s >= 0)
            def _():
                arrive(other - s)
                near_scores(other - s)

            @pl.when((s > 0) & (c + s < C))
            def _():
                arrive(other + s)
                near_scores(other + s)

    def round_(s, carry):
        has_left = (s < C) & (c - s >= 0)
        has_right = (s < C) & (c + s < C)

        @pl.when(has_left)
        def _():
            b = own - s
            arrive(b)

            @pl.when(c + 1 < C)
            def _():
                q_right(b).start()

            spread(b)

        @pl.when(has_right)
        def _():
            b = own + s
            arrive(b)

            @pl.when(c > 0)
            def _():
                q_left(b).start()

            spread(b)

        @pl.when(has_left)
        def _():
            near_scores(own - s)

        @pl.when(has_right)
        def _():
            near_scores(own + s)

        @pl.when(s == C - 1)
        def _():
            for t in range(parts):
                x_landed(t).wait_recv()
                f_copy(t).start()

            def step(t, carry):
                split_part(pts.at[m_x], m_x, t)
                score(a * C, C, m_x, t)
                return carry

            lax.fori_loop(0, parts, step, 0)

        @pl.when(s == C)
        def _():
            for t in range(parts):
                f_landed(t).wait_recv()

            def step(t, carry):
                split_part(pts.at[m_diag], m_diag, t)
                score(a * C, C, m_diag, t)
                return carry

            lax.fori_loop(0, parts, step, 0)

        across_blocks(s - 1)
        return carry

    lax.fori_loop(1, C + 1, round_, 0)
    for i in range(1, A):
        other = lax.rem(a + i, A) * C

        def far_across(t, carry):
            score(other, C, 2 * (1 - x) + lax.div(t, parts), lax.rem(t, parts))
            return carry

        lax.fori_loop(0, 2 * parts, far_across, 0)

    mx[m] = jnp.max(best[...], axis=0, keepdims=True)

    def m_copy(slot, to):
        return remote(mx.at[slot], mx.at[slot], m_send.at[to], m_recv.at[slot], base + to, c)

    for i in range(1, QUAD):
        m_copy(m, lax.rem(m + i, QUAD)).start()
    for i in range(1, QUAD):
        m_copy(lax.rem(m + i, QUAD), lax.rem(m + i, QUAD)).wait_recv()
    reached = jnp.maximum(jnp.maximum(mx[0], mx[1]), jnp.maximum(mx[2], mx[3]))
    cov[a] = jnp.maximum(cov_old[a], reached)

    def c_copy(slot, to):
        return remote(cov.at[slot], cov.at[slot], c_send.at[to], c_recv.at[slot], to * QUAD + m, c)

    for i in range(1, A):
        c_copy(a, lax.rem(a + i, A)).start()

    mine = m * NB + own

    def gains(b, carry):
        total = jnp.zeros((cap, 128), jnp.float32)
        for part in range(0, span, 128):
            total = total + jnp.maximum(sc[pl.ds(b * cap, cap), part : part + 128] - cov[a, :, part : part + 128], 0.0)
        gr[mine, pl.ds(b, 1)] = jnp.sum(total.T, axis=0, keepdims=True)
        return carry

    lax.fori_loop(0, NB, gains, 0)

    def g_copy(slot, dev):
        return remote(
            gr.at[slot], gr.at[slot], g_send.at[dev], g_recv.at[slot], lax.rem(dev, R), lax.div(dev, R)
        )

    def g_start(i, carry):
        g_copy(mine, lax.rem(me + i, ND)).start()
        return carry

    lax.fori_loop(1, ND, g_start, 0)

    for i in range(1, A):
        c_copy(lax.rem(a + i, A), lax.rem(a + i, A)).wait_recv()
    cov_out[...] = cov[...]

    def g_wait(i, carry):
        dev = lax.rem(me + i, ND)
        row, col = lax.rem(dev, R), lax.div(dev, R)
        g_copy(lax.rem(row, QUAD) * NB + lax.div(row, QUAD) * C + col, dev).wait_recv()
        return carry

    lax.fori_loop(1, ND, g_wait, 0)
    totals = jnp.concatenate(
        [jnp.sum(gr[i * NB : (i + 1) * NB], axis=0) for i in range(QUAD)], axis=0
    )
    spread_gain = jnp.dot(pick_owner, totals, precision=lax.Precision.HIGHEST, preferred_element_type=jnp.float32)
    gain_out[...] = jnp.sum(jnp.where(pick_slot, spread_gain, 0.0), axis=1, keepdims=True)

    for i in range(1, R):
        idx_copy(r, lax.rem(r + i, R)).wait_send()
    core_copy.wait_send()

    for s in range(parts):
        x_copy(s).wait_send()
        f_copy(s).wait_send()

    def left(s, carry):
        @pl.when(c - s >= 0)
        def _():
            @pl.when(c + 1 < C)
            def _():
                q_right(own - s).wait_send()

            for i in range(1, A):
                q_across(own - s, i).wait_send()

        @pl.when(c + s < C)
        def _():
            @pl.when(c > 0)
            def _():
                q_left(own + s).wait_send()

            @pl.when(s > 0)
            def _():
                for i in range(1, A):
                    q_across(own + s, i).wait_send()

        return carry

    lax.fori_loop(0, C, left, 0)
    for i in range(1, QUAD):
        m_copy(m, lax.rem(m + i, QUAD)).wait_send()
    for i in range(1, A):
        c_copy(a, lax.rem(a + i, A)).wait_send()

    def g_left(i, carry):
        g_copy(mine, lax.rem(me + i, ND)).wait_send()
        return carry

    lax.fori_loop(1, ND, g_left, 0)


def fused(R, C, slab_embed, coverage_old, sel_index, cand_index):
    rows, depth = slab_embed.shape
    ns, nk = sel_index.shape[0], cand_index.shape[0]
    A, ND = R // QUAD, R * C
    NB = A * C
    span = QUAD * rows
    mean = (ns + nk) * R / ND
    sent = int(-(-(mean + 3.7 * mean**0.5) // 8)) * 8
    cap = -(-sent // 32) * 32
    width = -(-(ns + nk) // 128) * 128
    parts = rows // 256
    f32, bf16, dma = jnp.float32, jnp.bfloat16, pltpu.SemaphoreType.DMA
    vmem = pl.BlockSpec(memory_space=pltpu.VMEM)
    coverage, gain, held = pl.pallas_call(
        functools.partial(kernel, R, C, cap, sent),
        out_shape=(
            jax.ShapeDtypeStruct((A, 1, span), f32),
            jax.ShapeDtypeStruct((nk, 1), f32),
            jax.ShapeDtypeStruct((1, 1), f32),
        ),
        in_specs=[vmem] * 4,
        out_specs=(vmem, vmem, vmem),
        scratch_shapes=[
            pltpu.VMEM((QUAD, rows, depth), f32),
            pltpu.VMEM((QUAD, rows, depth), bf16),
            pltpu.VMEM((QUAD, rows, depth), bf16),
            pltpu.VMEM((NB, cap, depth), f32),
            pltpu.VMEM((NB * cap, depth), bf16),
            pltpu.VMEM((NB * cap, depth), bf16),
            pltpu.VMEM((NB * cap, span), f32),
            pltpu.VMEM((R, 1, width), jnp.int32),
            pltpu.VMEM((NB * cap, 128), f32),
            pltpu.VMEM((8, span), f32),
            pltpu.VMEM((QUAD, 1, span), f32),
            pltpu.VMEM((A, 1, span), f32),
            pltpu.VMEM((ND, NB, cap), f32),
            dma((R,)), dma((R,)), dma((1,)), dma((1,)),
            dma((parts,)), dma((parts,)), dma((parts,)), dma((parts,)),
            dma((NB,)), dma((NB,)), dma((NB,)), dma((A - 1, NB)),
            dma((QUAD,)), dma((QUAD,)), dma((A,)), dma((A,)), dma((ND,)), dma((ND,)),
        ],
        compiler_params=pltpu.CompilerParams(
            collective_id=0, has_side_effects=True, vmem_limit_bytes=58 * 1024 * 1024
        ),
        cost_estimate=pl.CostEstimate(
            flops=6 * NB * cap * span * depth, bytes_accessed=rows * depth * 4, transcendentals=0
        ),
    )(
        slab_embed,
        coverage_old.reshape(A, 1, span),
        sel_index.reshape(1, ns),
        cand_index.reshape(1, nk),
    )
    return coverage.reshape(A * span), gain.reshape(nk), held[0, 0] > sent


def body(R, C, slab_embed, coverage_old, sel_index, cand_index):
    coverage, gain, crowded = fused(R, C, slab_embed, coverage_old, sel_index, cand_index)
    return lax.cond(
        crowded,
        lambda: any_draw(slab_embed, coverage_old, sel_index, cand_index),
        lambda: (coverage, gain),
    )


def solution(mesh):
    in_specs = (P(("col", "row"), None), P("col"), P("row"), P("row"))
    out_specs = (P("col"), P("row"))
    return jax.shard_map(
        functools.partial(body, mesh.shape["row"], mesh.shape["col"]),
        mesh=mesh, in_specs=in_specs, out_specs=out_specs, check_vma=False,
    )
```

```python
import functools

import jax
import jax.numpy as jnp
from jax import lax
from jax.experimental import pallas as pl
from jax.experimental.pallas import tpu as pltpu
from jax.sharding import PartitionSpec as P

MESH = pl.DeviceIdType.MESH
QUAD = 4
NT = (((1,), (1,)), ((), ()))


def similar(left, right):
    return lax.dot_general(
        left,
        right,
        (((1,), (1,)), ((), ())),
        precision=lax.Precision.HIGHEST,
        preferred_element_type=jnp.float32,
    )


def lookup(source, indices, first_row):
    position = indices - first_row
    inside = (position >= 0) & (position < source.shape[0])
    picked = jnp.take(source, jnp.clip(position, 0, source.shape[0] - 1), axis=0)
    return jnp.where(inside[:, None], picked, 0.0)


def any_draw(slab_embed, coverage_old, sel_index, cand_index):
    col_id = lax.axis_index("col")
    gathered = lax.all_gather(slab_embed, "row", axis=0, tiled=True)
    first_row = col_id * gathered.shape[0]
    selected, chosen = lax.psum(
        (lookup(gathered, sel_index, first_row), lookup(gathered, cand_index, first_row)), "col"
    )
    partial_value = jnp.max(similar(selected, gathered), axis=0)
    reached = lax.pmax(partial_value, "row")
    coverage = jnp.maximum(coverage_old, reached)
    gain_part = jnp.sum(jnp.maximum(similar(chosen, gathered) - coverage[None, :], 0.0), axis=1)
    return coverage, lax.psum(gain_part, "col")


def halves(value):
    high = value.astype(jnp.bfloat16)
    return high, (value - high.astype(jnp.float32)).astype(jnp.bfloat16)


def dot_nt(left, right):
    return lax.dot_general(left, right, NT, preferred_element_type=jnp.float32)


def kernel(
    R, C, cap, sent, slab, cov_old, sel, cand,
    cov_out, gain_out, flag_out,
    pts, ph, plo, qs, qh, ql, sc, idx, bias, best, mx, cov, gr,
    idx_send, idx_recv, core_send, core_recv, x_send, x_recv, f_send, f_recv,
    q_recv, ql_send, qr_send, qa_send, m_send, m_recv, c_send, c_recv, g_send, g_recv,
):
    A = R // QUAD
    NB = A * C
    ND = R * C
    rows = slab.shape[0]
    ns, nk = sel.shape[1], cand.shape[1]
    shift = rows.bit_length() - 1
    span = QUAD * rows
    r = lax.axis_index("row")
    c = lax.axis_index("col")
    me = c * R + r
    a = lax.div(r, QUAD)
    m = lax.rem(r, QUAD)
    x, h = lax.div(m, 2), lax.rem(m, 2)
    m_core = 2 * x + (1 - h)
    m_x = 2 * (1 - x) + h
    m_diag = 2 * (1 - x) + (1 - h)
    base = a * QUAD
    width = 256
    parts = rows // width

    def remote(src, dst, ssem, rsem, row, col):
        return pltpu.make_async_remote_copy(
            src_ref=src, dst_ref=dst, send_sem=ssem, recv_sem=rsem,
            device_id=(row, col), device_id_type=MESH,
        )

    barrier = pltpu.get_barrier_semaphore()

    def others(act):
        def wrap(value, size):
            return jnp.where(value >= size, value - size, value)

        for dr in range(1, R):
            act(wrap(r + dr, R), c)

        def column(dc, carry):
            col = wrap(c + dc, C)
            for dr in range(R):
                act(wrap(r + dr, R), col)
            return carry

        lax.fori_loop(1, C, column, 0)

    others(
        lambda row, col: pl.semaphore_signal(barrier, inc=1, device_id=(row, col), device_id_type=MESH)
    )
    idx[r] = jnp.full(idx.shape[1:], -1, jnp.int32)
    idx[r, :, 0:ns] = sel[...]
    idx[r, :, ns : ns + nk] = cand[...]
    pl.semaphore_wait(barrier, ND - 1)

    def idx_copy(slot, to):
        return remote(idx.at[slot], idx.at[slot], idx_send.at[to], idx_recv.at[slot], to, c)

    for i in range(1, R):
        idx_copy(r, lax.rem(r + i, R)).start()

    core_copy = remote(slab, pts.at[m], core_send.at[0], core_recv.at[0], base + m_core, c)
    core_copy.start()

    def x_copy(s):
        part = pl.ds(s * width, width)
        return remote(slab.at[part], pts.at[m, part], x_send.at[s], x_recv.at[s], base + m_x, c)

    def x_landed(s):
        part = pl.ds(s * width, width)
        return remote(slab.at[part], pts.at[m_x, part], x_send.at[s], x_recv.at[s], base + m_x, c)

    def f_copy(s):
        part = pl.ds(s * width, width)
        return remote(pts.at[m_x, part], pts.at[m_x, part], f_send.at[s], f_recv.at[s], base + m_core, c)

    def f_landed(s):
        part = pl.ds(s * width, width)
        return remote(pts.at[m_diag, part], pts.at[m_diag, part], f_send.at[s], f_recv.at[s], base + m_core, c)

    for s in range(parts):
        x_copy(s).start()

    def split_part(source, slot, s):
        part = pl.ds(s * width, width)
        high, low = halves(source[part])
        ph[slot, part] = high
        plo[slot, part] = low

    def split_points(source, slot):
        for s in range(parts):
            split_part(source, slot, s)

    if sent < cap:
        qs[:, sent:] = jnp.zeros((NB, cap - sent, qs.shape[2]), jnp.float32)
    best[...] = jnp.full(best.shape, -1e30, jnp.float32)
    split_points(slab, m)

    for i in range(1, R):
        idx_copy(lax.rem(r + i, R), lax.rem(r + i, R)).wait_recv()

    everything = jnp.concatenate([idx[j] for j in range(R)], axis=0)
    owner = lax.shift_right_logical(everything, shift)
    local = (everything - owner * rows).astype(jnp.float32)
    owner_sel, owner_cand = owner[:, 0:ns], owner[:, ns:]
    slot_id = lax.broadcasted_iota(jnp.int32, (cap, 128), 0).astype(jnp.float32)

    def place(owners, locals_, start, packed):
        n = owners.shape[1]
        mask = jnp.where(owners == me, 1.0, 0.0)
        before = lax.broadcasted_iota(jnp.int32, (n, n), 0) < lax.broadcasted_iota(jnp.int32, (n, n), 1)
        within = jnp.dot(
            mask.astype(jnp.bfloat16), before.astype(jnp.bfloat16), preferred_element_type=jnp.float32
        )
        for j in range(R):
            rank = jnp.where(mask[j : j + 1] > 0.0, within[j : j + 1] + start, -1.0)
            spot = locals_[j : j + 1] + 1.0
            for lane in range(0, n, 128):
                packed = packed + jnp.where(
                    rank[:, lane : lane + 128] == slot_id, spot[:, lane : lane + 128], 0.0
                )
            start = start + jnp.sum(mask[j : j + 1], axis=1, keepdims=True)
        return start, packed

    start, packed = place(
        owner_sel, local[:, 0:ns], jnp.zeros((1, 1), jnp.float32), jnp.zeros((cap, 128), jnp.float32)
    )
    start, packed = place(owner_cand, local[:, ns:], start, packed)
    packed = jnp.sum(packed, axis=1, keepdims=True)
    point = lax.broadcasted_iota(jnp.int32, (cap, rows), 1).astype(jnp.float32)
    pick = jnp.where(point == packed - 1.0, 1.0, 0.0).astype(jnp.bfloat16)
    own = a * C + c
    rows_owned = jnp.dot(pick, ph[m], preferred_element_type=jnp.float32) + jnp.dot(
        pick, plo[m], preferred_element_type=jnp.float32
    )
    qs[own, 0:sent] = rows_owned[0:sent]

    def q_copy(b, ssem, row, col):
        part = qs.at[b, pl.ds(0, sent)]
        return remote(part, part, ssem.at[b], q_recv.at[b], row, col)

    def q_right(b):
        return q_copy(b, qr_send, r, c + 1)

    def q_left(b):
        return q_copy(b, ql_send, r, c - 1)

    def q_across(b, i):
        return q_copy(b, qa_send.at[i - 1], (lax.rem(a + i, A)) * QUAD + m, c)

    def spread(b):
        for i in range(1, A):
            q_across(b, i).start()

    @pl.when(c + 1 < C)
    def _():
        q_right(own).start()

    @pl.when(c > 0)
    def _():
        q_left(own).start()

    spread(own)

    def split_block(b):
        high, low = halves(qs[b])
        qh[pl.ds(b * cap, cap)] = high
        ql[pl.ds(b * cap, cap)] = low

    def score(first, count, slot, s):
        part = pl.ds(s * width, width)
        out = pl.ds(slot * rows + s * width, width)
        block = pl.ds(first * cap, count * cap)
        high, low = ph[slot, part], plo[slot, part]
        n = count * cap
        both = dot_nt(jnp.concatenate([qh[block], ql[block]], axis=0), high)
        value = both[0:n] + both[n:] + dot_nt(qh[block], low)
        sc[block, out] = value
        shift_by = bias[block]
        top = jnp.concatenate(
            [
                jnp.max(
                    (value[:, lane : lane + 128] + shift_by).reshape(n // 8, 8, 128), axis=0
                )
                for lane in range(0, width, 128)
            ],
            axis=1,
        )
        best[:, out] = jnp.maximum(best[:, out], top)

    def near_scores(b):
        split_block(b)

        def step(t, carry):
            score(b, 1, 2 * x + lax.div(t, parts), lax.rem(t, parts))
            return carry

        lax.fori_loop(0, 2 * parts, step, 0)

    core_landed = remote(slab, pts.at[m_core], core_send.at[0], core_recv.at[0], base + m_core, c)
    core_landed.wait_recv()
    split_points(pts.at[m_core], m_core)
    def mark(b, carry):
        owner_id = lax.rem(b, C) * R + lax.div(b, C) * QUAD + m
        count = jnp.sum(
            jnp.sum(jnp.where(owner_sel == owner_id, 1.0, 0.0), axis=1, keepdims=True), axis=0, keepdims=True
        )
        bias[pl.ds(b * cap, cap)] = jnp.where(slot_id < count, 0.0, -1e30)
        return carry

    lax.fori_loop(0, NB, mark, 0)
    near_scores(own)

    square = (nk, nk)
    across, down = lax.broadcasted_iota(jnp.int32, square, 1), lax.broadcasted_iota(jnp.int32, square, 0)
    mine_row = lax.shift_right_logical(cand[...], shift).astype(jnp.float32)
    mine_owner = jnp.sum(jnp.where(across == down, mine_row, 0.0), axis=1, keepdims=True).astype(jnp.int32)
    wide = owner_cand.shape[1]
    earlier = lax.broadcasted_iota(jnp.int32, (nk, wide), 1) < lax.broadcasted_iota(jnp.int32, (nk, wide), 0)
    same_total = jnp.zeros((nk, 128), jnp.float32)
    for j in range(R):
        same = jnp.where(owner_sel[j : j + 1] == mine_owner, 1.0, 0.0)
        for lane in range(0, ns, 128):
            same_total = same_total + same[:, lane : lane + 128]
        counted = (j < r) | ((j == r) & earlier)
        same = jnp.where(counted & (owner_cand[j : j + 1] == mine_owner), 1.0, 0.0)
        for lane in range(0, wide, 128):
            same_total = same_total + same[:, lane : lane + 128]
    rank = jnp.sum(same_total, axis=1, keepdims=True)
    row_of = lax.rem(mine_owner, R)
    flat = lax.rem(row_of, QUAD) * NB + lax.div(row_of, QUAD) * C + lax.div(mine_owner, R)
    pick_owner = jnp.where(lax.broadcasted_iota(jnp.int32, (nk, ND), 1) == flat, 1.0, 0.0)
    pick_slot = lax.broadcasted_iota(jnp.int32, (nk, cap), 1).astype(jnp.float32) == rank

    dev_id = lax.broadcasted_iota(jnp.int32, (ND, 1), 0)
    held = jnp.zeros((ND, 128), jnp.float32)
    for j in range(R):
        for lane in range(0, ns + wide, 128):
            held = held + jnp.where(owner[j : j + 1, lane : lane + 128] == dev_id, 1.0, 0.0)
    held = jnp.sum(held, axis=1, keepdims=True)
    flag_out[...] = jnp.max(held, axis=0, keepdims=True)

    def arrive(b):
        q_copy(b, ql_send, r, c).wait_recv()

    last = jnp.where(2 * c < C, C - 1, 0)
    first = jnp.where(2 * c < C, 0, 1)

    def across_blocks(s):
        for i in range(1, A):
            other = lax.rem(a + i, A) * C + c

            @pl.when((c - s >= 0) & (c - s != last))
            def _():
                arrive(other - s)
                near_scores(other - s)

            @pl.when((s > 0) & (c + s < C) & (c + s != last))
            def _():
                arrive(other + s)
                near_scores(other + s)

    def round_(s, carry):
        has_left = (s < C) & (c - s >= 0)
        has_right = (s < C) & (c + s < C)

        @pl.when(has_left)
        def _():
            b = own - s
            arrive(b)

            @pl.when(c + 1 < C)
            def _():
                q_right(b).start()

            spread(b)

        @pl.when(has_right)
        def _():
            b = own + s
            arrive(b)

            @pl.when(c > 0)
            def _():
                q_left(b).start()

            spread(b)

        @pl.when(has_left)
        def _():
            near_scores(own - s)

        @pl.when(has_right)
        def _():
            near_scores(own + s)

        @pl.when(s == C - 1)
        def _():
            for t in range(parts):
                x_landed(t).wait_recv()
                f_copy(t).start()

            def step(t, carry):
                split_part(pts.at[m_x], m_x, t)
                score(a * C, C, m_x, t)
                return carry

            lax.fori_loop(0, parts, step, 0)

        @pl.when(s == C)
        def _():
            for t in range(parts):
                f_landed(t).wait_recv()

            def step(t, carry):
                split_part(pts.at[m_diag], m_diag, t)
                score(a * C, C, m_diag, t)
                return carry

            lax.fori_loop(0, parts, step, 0)

        across_blocks(s - 1)
        return carry

    lax.fori_loop(1, C + 1, round_, 0)
    for i in range(1, A):
        other = lax.rem(a + i, A) * C

        def far_across(t, carry):
            score(other + first, C - 1, 2 * (1 - x) + lax.div(t, parts), lax.rem(t, parts))
            return carry

        lax.fori_loop(0, 2 * parts, far_across, 0)

    for i in range(1, A):
        other = lax.rem(a + i, A) * C
        arrive(other + last)
        split_block(other + last)

        def last_scores(t, carry):
            score(other + last, 1, lax.div(t, parts), lax.rem(t, parts))
            return carry

        lax.fori_loop(0, QUAD * parts, last_scores, 0)

    mx[m] = jnp.max(best[...], axis=0, keepdims=True)

    def m_copy(slot, to):
        return remote(mx.at[slot], mx.at[slot], m_send.at[to], m_recv.at[slot], base + to, c)

    for i in range(1, QUAD):
        m_copy(m, lax.rem(m + i, QUAD)).start()
    for i in range(1, QUAD):
        m_copy(lax.rem(m + i, QUAD), lax.rem(m + i, QUAD)).wait_recv()
    reached = jnp.maximum(jnp.maximum(mx[0], mx[1]), jnp.maximum(mx[2], mx[3]))
    cov[a] = jnp.maximum(cov_old[a], reached)

    def c_copy(slot, to):
        return remote(cov.at[slot], cov.at[slot], c_send.at[to], c_recv.at[slot], to * QUAD + m, c)

    for i in range(1, A):
        c_copy(a, lax.rem(a + i, A)).start()

    mine = m * NB + own

    def gains(b, carry):
        total = jnp.zeros((cap, 128), jnp.float32)
        for part in range(0, span, 128):
            total = total + jnp.maximum(sc[pl.ds(b * cap, cap), part : part + 128] - cov[a, :, part : part + 128], 0.0)
        gr[mine, pl.ds(b, 1)] = jnp.sum(total.T, axis=0, keepdims=True)
        return carry

    lax.fori_loop(0, NB, gains, 0)

    def g_copy(part, row, col):
        return remote(part, part, g_send.at[0], g_recv.at[0], row, col)

    others(lambda row, col: g_copy(gr.at[mine], row, col).start())

    for i in range(1, A):
        c_copy(lax.rem(a + i, A), lax.rem(a + i, A)).wait_recv()
    cov_out[...] = cov[...]

    every = g_copy(gr.at[pl.ds(0, ND - 1)], r, c)
    every.wait_recv()
    totals = jnp.concatenate(
        [jnp.sum(gr[i * NB : (i + 1) * NB], axis=0) for i in range(QUAD)], axis=0
    )
    spread_gain = jnp.dot(pick_owner, totals, precision=lax.Precision.HIGHEST, preferred_element_type=jnp.float32)
    gain_out[...] = jnp.sum(jnp.where(pick_slot, spread_gain, 0.0), axis=1, keepdims=True)

    for i in range(1, R):
        idx_copy(r, lax.rem(r + i, R)).wait_send()
    core_copy.wait_send()

    for s in range(parts):
        x_copy(s).wait_send()
        f_copy(s).wait_send()

    def left(s, carry):
        @pl.when(c - s >= 0)
        def _():
            @pl.when(c + 1 < C)
            def _():
                q_right(own - s).wait_send()

            for i in range(1, A):
                q_across(own - s, i).wait_send()

        @pl.when(c + s < C)
        def _():
            @pl.when(c > 0)
            def _():
                q_left(own + s).wait_send()

            @pl.when(s > 0)
            def _():
                for i in range(1, A):
                    q_across(own + s, i).wait_send()

        return carry

    lax.fori_loop(0, C, left, 0)
    for i in range(1, QUAD):
        m_copy(m, lax.rem(m + i, QUAD)).wait_send()
    for i in range(1, A):
        c_copy(a, lax.rem(a + i, A)).wait_send()

    every.wait_send()


def fused(R, C, slab_embed, coverage_old, sel_index, cand_index):
    rows, depth = slab_embed.shape
    ns, nk = sel_index.shape[0], cand_index.shape[0]
    A, ND = R // QUAD, R * C
    NB = A * C
    span = QUAD * rows
    mean = (ns + nk) * R / ND
    sent = int(-(-(mean + 3.7 * mean**0.5) // 8)) * 8
    cap = -(-sent // 32) * 32
    width = -(-(ns + nk) // 128) * 128
    parts = rows // 256
    f32, bf16, dma = jnp.float32, jnp.bfloat16, pltpu.SemaphoreType.DMA
    vmem = pl.BlockSpec(memory_space=pltpu.VMEM)
    coverage, gain, held = pl.pallas_call(
        functools.partial(kernel, R, C, cap, sent),
        out_shape=(
            jax.ShapeDtypeStruct((A, 1, span), f32),
            jax.ShapeDtypeStruct((nk, 1), f32),
            jax.ShapeDtypeStruct((1, 1), f32),
        ),
        in_specs=[vmem] * 4,
        out_specs=(vmem, vmem, vmem),
        scratch_shapes=[
            pltpu.VMEM((QUAD, rows, depth), f32),
            pltpu.VMEM((QUAD, rows, depth), bf16),
            pltpu.VMEM((QUAD, rows, depth), bf16),
            pltpu.VMEM((NB, cap, depth), f32),
            pltpu.VMEM((NB * cap, depth), bf16),
            pltpu.VMEM((NB * cap, depth), bf16),
            pltpu.VMEM((NB * cap, span), f32),
            pltpu.VMEM((R, 1, width), jnp.int32),
            pltpu.VMEM((NB * cap, 128), f32),
            pltpu.VMEM((8, span), f32),
            pltpu.VMEM((QUAD, 1, span), f32),
            pltpu.VMEM((A, 1, span), f32),
            pltpu.VMEM((ND, NB, cap), f32),
            dma((R,)), dma((R,)), dma((1,)), dma((1,)),
            dma((parts,)), dma((parts,)), dma((parts,)), dma((parts,)),
            dma((NB,)), dma((NB,)), dma((NB,)), dma((A - 1, NB)),
            dma((QUAD,)), dma((QUAD,)), dma((A,)), dma((A,)), dma((1,)), dma((1,)),
        ],
        compiler_params=pltpu.CompilerParams(
            collective_id=0, has_side_effects=True, vmem_limit_bytes=58 * 1024 * 1024
        ),
        cost_estimate=pl.CostEstimate(
            flops=6 * NB * cap * span * depth, bytes_accessed=rows * depth * 4, transcendentals=0
        ),
    )(
        slab_embed,
        coverage_old.reshape(A, 1, span),
        sel_index.reshape(1, ns),
        cand_index.reshape(1, nk),
    )
    return coverage.reshape(A * span), gain.reshape(nk), held[0, 0] > sent


def body(R, C, slab_embed, coverage_old, sel_index, cand_index):
    coverage, gain, crowded = fused(R, C, slab_embed, coverage_old, sel_index, cand_index)
    return lax.cond(
        crowded,
        lambda: any_draw(slab_embed, coverage_old, sel_index, cand_index),
        lambda: (coverage, gain),
    )


def solution(mesh):
    in_specs = (P(("col", "row"), None), P("col"), P("row"), P("row"))
    out_specs = (P("col"), P("row"))
    return jax.shard_map(
        functools.partial(body, mesh.shape["row"], mesh.shape["col"]),
        mesh=mesh, in_specs=in_specs, out_specs=out_specs, check_vma=False,
    )
```

```python
import functools

import jax
import jax.numpy as jnp
from jax import lax
from jax.experimental import pallas as pl
from jax.experimental.pallas import tpu as pltpu
from jax.sharding import PartitionSpec as P

MESH = pl.DeviceIdType.MESH
QUAD = 4
NT = (((1,), (1,)), ((), ()))


def similar(left, right):
    return lax.dot_general(
        left,
        right,
        (((1,), (1,)), ((), ())),
        precision=lax.Precision.HIGHEST,
        preferred_element_type=jnp.float32,
    )


def lookup(source, indices, first_row):
    position = indices - first_row
    inside = (position >= 0) & (position < source.shape[0])
    picked = jnp.take(source, jnp.clip(position, 0, source.shape[0] - 1), axis=0)
    return jnp.where(inside[:, None], picked, 0.0)


def any_draw(slab_embed, coverage_old, sel_index, cand_index):
    col_id = lax.axis_index("col")
    gathered = lax.all_gather(slab_embed, "row", axis=0, tiled=True)
    first_row = col_id * gathered.shape[0]
    selected, chosen = lax.psum(
        (lookup(gathered, sel_index, first_row), lookup(gathered, cand_index, first_row)), "col"
    )
    partial_value = jnp.max(similar(selected, gathered), axis=0)
    reached = lax.pmax(partial_value, "row")
    coverage = jnp.maximum(coverage_old, reached)
    gain_part = jnp.sum(jnp.maximum(similar(chosen, gathered) - coverage[None, :], 0.0), axis=1)
    return coverage, lax.psum(gain_part, "col")


def halves(value):
    high = value.astype(jnp.bfloat16)
    return high, (value - high.astype(jnp.float32)).astype(jnp.bfloat16)


def dot(left, right):
    return jnp.dot(left, right, preferred_element_type=jnp.float32)


def dot_nt(left, right):
    return lax.dot_general(left, right, NT, preferred_element_type=jnp.float32)


def kernel(
    R, C, cap, sent, slab, cov_old, sel, cand,
    cov_out, gain_out, flag_out,
    pts, ph, plo, qs, qh, ql, sc, idx, bias, best, mx, cov, gr,
    idx_send, idx_recv, core_send, core_recv, x_send, x_recv, f_send, f_recv,
    q_recv, ql_send, qr_send, qa_send, m_send, m_recv, c_send, c_recv, g_send, g_recv,
):
    A = R // QUAD
    NB = A * C
    ND = R * C
    rows = slab.shape[0]
    ns, nk = sel.shape[1], cand.shape[1]
    shift = rows.bit_length() - 1
    span = QUAD * rows
    r = lax.axis_index("row")
    c = lax.axis_index("col")
    me = c * R + r
    a = lax.div(r, QUAD)
    m = lax.rem(r, QUAD)
    x, h = lax.div(m, 2), lax.rem(m, 2)
    m_core = 2 * x + (1 - h)
    m_x = 2 * (1 - x) + h
    m_diag = 2 * (1 - x) + (1 - h)
    base = a * QUAD
    width = 256
    parts = rows // width

    def remote(src, dst, ssem, rsem, row, col):
        return pltpu.make_async_remote_copy(
            src_ref=src, dst_ref=dst, send_sem=ssem, recv_sem=rsem,
            device_id=(row, col), device_id_type=MESH,
        )

    barrier = pltpu.get_barrier_semaphore()

    def others(act):
        def wrap(value, size):
            return jnp.where(value >= size, value - size, value)

        for dr in range(1, R):
            act(wrap(r + dr, R), c)

        def column(dc, carry):
            col = wrap(c + dc, C)
            for dr in range(R):
                act(wrap(r + dr, R), col)
            return carry

        lax.fori_loop(1, C, column, 0)

    others(
        lambda row, col: pl.semaphore_signal(barrier, inc=1, device_id=(row, col), device_id_type=MESH)
    )
    idx[r] = jnp.full(idx.shape[1:], -1, jnp.int32)
    idx[r, :, 0:ns] = sel[...]
    idx[r, :, ns : ns + nk] = cand[...]
    pl.semaphore_wait(barrier, ND - 1)

    def idx_copy(slot, to):
        return remote(idx.at[slot], idx.at[slot], idx_send.at[to], idx_recv.at[slot], to, c)

    for i in range(1, R):
        idx_copy(r, lax.rem(r + i, R)).start()

    core_copy = remote(slab, pts.at[m], core_send.at[0], core_recv.at[0], base + m_core, c)
    core_copy.start()

    def x_copy(s):
        part = pl.ds(s * width, width)
        return remote(slab.at[part], pts.at[m, part], x_send.at[s], x_recv.at[s], base + m_x, c)

    def x_landed(s):
        part = pl.ds(s * width, width)
        return remote(slab.at[part], pts.at[m_x, part], x_send.at[s], x_recv.at[s], base + m_x, c)

    def f_copy(s):
        part = pl.ds(s * width, width)
        return remote(pts.at[m_x, part], pts.at[m_x, part], f_send.at[s], f_recv.at[s], base + m_core, c)

    def f_landed(s):
        part = pl.ds(s * width, width)
        return remote(pts.at[m_diag, part], pts.at[m_diag, part], f_send.at[s], f_recv.at[s], base + m_core, c)

    for s in range(parts):
        x_copy(s).start()

    def split_part(source, slot, s):
        part = pl.ds(s * width, width)
        high, low = halves(source[part].T)
        ph[slot, s] = high
        plo[slot, s] = low

    def split_points(source, slot):
        for s in range(parts):
            split_part(source, slot, s)

    if sent < cap:
        qs[:, sent:] = jnp.zeros((NB, cap - sent, qs.shape[2]), jnp.float32)
    best[...] = jnp.full(best.shape, -1e30, jnp.float32)
    split_points(slab, m)

    for i in range(1, R):
        idx_copy(lax.rem(r + i, R), lax.rem(r + i, R)).wait_recv()

    everything = jnp.concatenate([idx[j] for j in range(R)], axis=0)
    owner = lax.shift_right_logical(everything, shift)
    local = (everything - owner * rows).astype(jnp.float32)
    owner_sel, owner_cand = owner[:, 0:ns], owner[:, ns:]
    slot_id = lax.broadcasted_iota(jnp.int32, (cap, 128), 0).astype(jnp.float32)

    def place(owners, locals_, start, packed):
        n = owners.shape[1]
        mask = jnp.where(owners == me, 1.0, 0.0)
        before = lax.broadcasted_iota(jnp.int32, (n, n), 0) < lax.broadcasted_iota(jnp.int32, (n, n), 1)
        within = jnp.dot(
            mask.astype(jnp.bfloat16), before.astype(jnp.bfloat16), preferred_element_type=jnp.float32
        )
        for j in range(R):
            rank = jnp.where(mask[j : j + 1] > 0.0, within[j : j + 1] + start, -1.0)
            spot = locals_[j : j + 1] + 1.0
            for lane in range(0, n, 128):
                packed = packed + jnp.where(
                    rank[:, lane : lane + 128] == slot_id, spot[:, lane : lane + 128], 0.0
                )
            start = start + jnp.sum(mask[j : j + 1], axis=1, keepdims=True)
        return start, packed

    start, packed = place(
        owner_sel, local[:, 0:ns], jnp.zeros((1, 1), jnp.float32), jnp.zeros((cap, 128), jnp.float32)
    )
    start, packed = place(owner_cand, local[:, ns:], start, packed)
    packed = jnp.sum(packed, axis=1, keepdims=True)
    point = lax.broadcasted_iota(jnp.int32, (cap, rows), 1).astype(jnp.float32)
    pick = jnp.where(point == packed - 1.0, 1.0, 0.0).astype(jnp.bfloat16)
    own = a * C + c
    rows_owned = jnp.zeros((cap, qs.shape[2]), jnp.float32)
    for s in range(parts):
        chosen = pick[:, s * width : (s + 1) * width]
        rows_owned = rows_owned + (dot_nt(chosen, ph[m, s]) + dot_nt(chosen, plo[m, s]))
    qs[own, 0:sent] = rows_owned[0:sent]

    def q_copy(b, ssem, row, col):
        part = qs.at[b, pl.ds(0, sent)]
        return remote(part, part, ssem.at[b], q_recv.at[b], row, col)

    def q_right(b):
        return q_copy(b, qr_send, r, c + 1)

    def q_left(b):
        return q_copy(b, ql_send, r, c - 1)

    def q_across(b, i):
        return q_copy(b, qa_send.at[i - 1], (lax.rem(a + i, A)) * QUAD + m, c)

    def spread(b):
        for i in range(1, A):
            q_across(b, i).start()

    @pl.when(c + 1 < C)
    def _():
        q_right(own).start()

    @pl.when(c > 0)
    def _():
        q_left(own).start()

    spread(own)

    def split_block(b):
        high, low = halves(qs[b])
        qh[pl.ds(b * cap, cap)] = high
        ql[pl.ds(b * cap, cap)] = low

    def score(first, count, slot, s):
        out = pl.ds(slot * rows + s * width, width)
        block = pl.ds(first * cap, count * cap)
        high, low = ph[slot, s], plo[slot, s]
        n = count * cap
        both = dot(jnp.concatenate([qh[block], ql[block]], axis=0), high)
        value = both[0:n] + both[n:] + dot(qh[block], low)
        sc[block, out] = value
        shift_by = bias[block]
        top = jnp.concatenate(
            [
                jnp.max(
                    (value[:, lane : lane + 128] + shift_by).reshape(n // 8, 8, 128), axis=0
                )
                for lane in range(0, width, 128)
            ],
            axis=1,
        )
        best[:, out] = jnp.maximum(best[:, out], top)

    def near_scores(b):
        split_block(b)

        def step(t, carry):
            score(b, 1, 2 * x + lax.div(t, parts), lax.rem(t, parts))
            return carry

        lax.fori_loop(0, 2 * parts, step, 0)

    core_landed = remote(slab, pts.at[m_core], core_send.at[0], core_recv.at[0], base + m_core, c)
    core_landed.wait_recv()
    split_points(pts.at[m_core], m_core)
    def mark(b, carry):
        owner_id = lax.rem(b, C) * R + lax.div(b, C) * QUAD + m
        count = jnp.sum(
            jnp.sum(jnp.where(owner_sel == owner_id, 1.0, 0.0), axis=1, keepdims=True), axis=0, keepdims=True
        )
        bias[pl.ds(b * cap, cap)] = jnp.where(slot_id < count, 0.0, -1e30)
        return carry

    lax.fori_loop(0, NB, mark, 0)
    near_scores(own)

    square = (nk, nk)
    across, down = lax.broadcasted_iota(jnp.int32, square, 1), lax.broadcasted_iota(jnp.int32, square, 0)
    mine_row = lax.shift_right_logical(cand[...], shift).astype(jnp.float32)
    mine_owner = jnp.sum(jnp.where(across == down, mine_row, 0.0), axis=1, keepdims=True).astype(jnp.int32)
    wide = owner_cand.shape[1]
    earlier = lax.broadcasted_iota(jnp.int32, (nk, wide), 1) < lax.broadcasted_iota(jnp.int32, (nk, wide), 0)
    same_total = jnp.zeros((nk, 128), jnp.float32)
    for j in range(R):
        same = jnp.where(owner_sel[j : j + 1] == mine_owner, 1.0, 0.0)
        for lane in range(0, ns, 128):
            same_total = same_total + same[:, lane : lane + 128]
        counted = (j < r) | ((j == r) & earlier)
        same = jnp.where(counted & (owner_cand[j : j + 1] == mine_owner), 1.0, 0.0)
        for lane in range(0, wide, 128):
            same_total = same_total + same[:, lane : lane + 128]
    rank = jnp.sum(same_total, axis=1, keepdims=True)
    row_of = lax.rem(mine_owner, R)
    flat = lax.rem(row_of, QUAD) * NB + lax.div(row_of, QUAD) * C + lax.div(mine_owner, R)
    pick_owner = jnp.where(lax.broadcasted_iota(jnp.int32, (nk, ND), 1) == flat, 1.0, 0.0)
    pick_slot = lax.broadcasted_iota(jnp.int32, (nk, cap), 1).astype(jnp.float32) == rank

    dev_id = lax.broadcasted_iota(jnp.int32, (ND, 1), 0)
    held = jnp.zeros((ND, 128), jnp.float32)
    for j in range(R):
        for lane in range(0, ns + wide, 128):
            held = held + jnp.where(owner[j : j + 1, lane : lane + 128] == dev_id, 1.0, 0.0)
    held = jnp.sum(held, axis=1, keepdims=True)
    flag_out[...] = jnp.max(held, axis=0, keepdims=True)

    def arrive(b):
        q_copy(b, ql_send, r, c).wait_recv()

    last = jnp.where(2 * c < C, C - 1, 0)
    first = jnp.where(2 * c < C, 0, 1)

    def across_blocks(s):
        for i in range(1, A):
            other = lax.rem(a + i, A) * C + c

            @pl.when((c - s >= 0) & (c - s != last))
            def _():
                arrive(other - s)
                near_scores(other - s)

            @pl.when((s > 0) & (c + s < C) & (c + s != last))
            def _():
                arrive(other + s)
                near_scores(other + s)

    def round_(s, carry):
        has_left = (s < C) & (c - s >= 0)
        has_right = (s < C) & (c + s < C)

        @pl.when(has_left)
        def _():
            b = own - s
            arrive(b)

            @pl.when(c + 1 < C)
            def _():
                q_right(b).start()

            spread(b)

        @pl.when(has_right)
        def _():
            b = own + s
            arrive(b)

            @pl.when(c > 0)
            def _():
                q_left(b).start()

            spread(b)

        @pl.when(has_left)
        def _():
            near_scores(own - s)

        @pl.when(has_right)
        def _():
            near_scores(own + s)

        @pl.when(s == C - 1)
        def _():
            for t in range(parts):
                x_landed(t).wait_recv()
                f_copy(t).start()

            def step(t, carry):
                split_part(pts.at[m_x], m_x, t)
                score(a * C, C, m_x, t)
                return carry

            lax.fori_loop(0, parts, step, 0)

        @pl.when(s == C)
        def _():
            for t in range(parts):
                f_landed(t).wait_recv()

            def step(t, carry):
                split_part(pts.at[m_diag], m_diag, t)
                score(a * C, C, m_diag, t)
                return carry

            lax.fori_loop(0, parts, step, 0)

        across_blocks(s - 1)
        return carry

    lax.fori_loop(1, C + 1, round_, 0)
    for i in range(1, A):
        other = lax.rem(a + i, A) * C

        def far_across(t, carry):
            score(other + first, C - 1, 2 * (1 - x) + lax.div(t, parts), lax.rem(t, parts))
            return carry

        lax.fori_loop(0, 2 * parts, far_across, 0)

    for i in range(1, A):
        other = lax.rem(a + i, A) * C
        arrive(other + last)
        split_block(other + last)

        def last_scores(t, carry):
            score(other + last, 1, lax.div(t, parts), lax.rem(t, parts))
            return carry

        lax.fori_loop(0, QUAD * parts, last_scores, 0)

    mx[m] = jnp.max(best[...], axis=0, keepdims=True)

    def m_copy(slot, to):
        return remote(mx.at[slot], mx.at[slot], m_send.at[to], m_recv.at[slot], base + to, c)

    for i in range(1, QUAD):
        m_copy(m, lax.rem(m + i, QUAD)).start()
    for i in range(1, QUAD):
        m_copy(lax.rem(m + i, QUAD), lax.rem(m + i, QUAD)).wait_recv()
    reached = jnp.maximum(jnp.maximum(mx[0], mx[1]), jnp.maximum(mx[2], mx[3]))
    cov[a] = jnp.maximum(cov_old[a], reached)

    def c_copy(slot, to):
        return remote(cov.at[slot], cov.at[slot], c_send.at[to], c_recv.at[slot], to * QUAD + m, c)

    for i in range(1, A):
        c_copy(a, lax.rem(a + i, A)).start()

    mine = m * NB + own

    def gains(b, carry):
        total = jnp.zeros((cap, 128), jnp.float32)
        for part in range(0, span, 128):
            total = total + jnp.maximum(sc[pl.ds(b * cap, cap), part : part + 128] - cov[a, :, part : part + 128], 0.0)
        gr[mine, pl.ds(b, 1)] = jnp.sum(total.T, axis=0, keepdims=True)
        return carry

    lax.fori_loop(0, NB, gains, 0)

    def g_copy(part, row, col):
        return remote(part, part, g_send.at[0], g_recv.at[0], row, col)

    others(lambda row, col: g_copy(gr.at[mine], row, col).start())

    for i in range(1, A):
        c_copy(lax.rem(a + i, A), lax.rem(a + i, A)).wait_recv()
    cov_out[...] = cov[...]

    every = g_copy(gr.at[pl.ds(0, ND - 1)], r, c)
    every.wait_recv()
    totals = jnp.concatenate(
        [jnp.sum(gr[i * NB : (i + 1) * NB], axis=0) for i in range(QUAD)], axis=0
    )
    spread_gain = jnp.dot(pick_owner, totals, precision=lax.Precision.HIGHEST, preferred_element_type=jnp.float32)
    gain_out[...] = jnp.sum(jnp.where(pick_slot, spread_gain, 0.0), axis=1, keepdims=True)

    for i in range(1, R):
        idx_copy(r, lax.rem(r + i, R)).wait_send()
    core_copy.wait_send()

    for s in range(parts):
        x_copy(s).wait_send()
        f_copy(s).wait_send()

    def left(s, carry):
        @pl.when(c - s >= 0)
        def _():
            @pl.when(c + 1 < C)
            def _():
                q_right(own - s).wait_send()

            for i in range(1, A):
                q_across(own - s, i).wait_send()

        @pl.when(c + s < C)
        def _():
            @pl.when(c > 0)
            def _():
                q_left(own + s).wait_send()

            @pl.when(s > 0)
            def _():
                for i in range(1, A):
                    q_across(own + s, i).wait_send()

        return carry

    lax.fori_loop(0, C, left, 0)
    for i in range(1, QUAD):
        m_copy(m, lax.rem(m + i, QUAD)).wait_send()
    for i in range(1, A):
        c_copy(a, lax.rem(a + i, A)).wait_send()

    every.wait_send()


def fused(R, C, slab_embed, coverage_old, sel_index, cand_index):
    rows, depth = slab_embed.shape
    ns, nk = sel_index.shape[0], cand_index.shape[0]
    A, ND = R // QUAD, R * C
    NB = A * C
    span = QUAD * rows
    mean = (ns + nk) * R / ND
    sent = int(-(-(mean + 3.7 * mean**0.5) // 8)) * 8
    cap = -(-sent // 32) * 32
    width = -(-(ns + nk) // 128) * 128
    parts = rows // 256
    f32, bf16, dma = jnp.float32, jnp.bfloat16, pltpu.SemaphoreType.DMA
    vmem = pl.BlockSpec(memory_space=pltpu.VMEM)
    coverage, gain, held = pl.pallas_call(
        functools.partial(kernel, R, C, cap, sent),
        out_shape=(
            jax.ShapeDtypeStruct((A, 1, span), f32),
            jax.ShapeDtypeStruct((nk, 1), f32),
            jax.ShapeDtypeStruct((1, 1), f32),
        ),
        in_specs=[vmem] * 4,
        out_specs=(vmem, vmem, vmem),
        scratch_shapes=[
            pltpu.VMEM((QUAD, rows, depth), f32),
            pltpu.VMEM((QUAD, parts, depth, 256), bf16),
            pltpu.VMEM((QUAD, parts, depth, 256), bf16),
            pltpu.VMEM((NB, cap, depth), f32),
            pltpu.VMEM((NB * cap, depth), bf16),
            pltpu.VMEM((NB * cap, depth), bf16),
            pltpu.VMEM((NB * cap, span), f32),
            pltpu.VMEM((R, 1, width), jnp.int32),
            pltpu.VMEM((NB * cap, 128), f32),
            pltpu.VMEM((8, span), f32),
            pltpu.VMEM((QUAD, 1, span), f32),
            pltpu.VMEM((A, 1, span), f32),
            pltpu.VMEM((ND, NB, cap), f32),
            dma((R,)), dma((R,)), dma((1,)), dma((1,)),
            dma((parts,)), dma((parts,)), dma((parts,)), dma((parts,)),
            dma((NB,)), dma((NB,)), dma((NB,)), dma((A - 1, NB)),
            dma((QUAD,)), dma((QUAD,)), dma((A,)), dma((A,)), dma((1,)), dma((1,)),
        ],
        compiler_params=pltpu.CompilerParams(
            collective_id=0, has_side_effects=True, vmem_limit_bytes=58 * 1024 * 1024
        ),
        cost_estimate=pl.CostEstimate(
            flops=6 * NB * cap * span * depth, bytes_accessed=rows * depth * 4, transcendentals=0
        ),
    )(
        slab_embed,
        coverage_old.reshape(A, 1, span),
        sel_index.reshape(1, ns),
        cand_index.reshape(1, nk),
    )
    return coverage.reshape(A * span), gain.reshape(nk), held[0, 0] > sent


def body(R, C, slab_embed, coverage_old, sel_index, cand_index):
    coverage, gain, crowded = fused(R, C, slab_embed, coverage_old, sel_index, cand_index)
    return lax.cond(
        crowded,
        lambda: any_draw(slab_embed, coverage_old, sel_index, cand_index),
        lambda: (coverage, gain),
    )


def solution(mesh):
    in_specs = (P(("col", "row"), None), P("col"), P("row"), P("row"))
    out_specs = (P("col"), P("row"))
    return jax.shard_map(
        functools.partial(body, mesh.shape["row"], mesh.shape["col"]),
        mesh=mesh, in_specs=in_specs, out_specs=out_specs, check_vma=False,
    )
```

```python
import functools

import jax
import jax.numpy as jnp
from jax import lax
from jax.experimental import pallas as pl
from jax.experimental.pallas import tpu as pltpu
from jax.sharding import PartitionSpec as P

MESH = pl.DeviceIdType.MESH
QUAD = 4
NT = (((1,), (1,)), ((), ()))


def similar(left, right):
    return lax.dot_general(
        left,
        right,
        (((1,), (1,)), ((), ())),
        precision=lax.Precision.HIGHEST,
        preferred_element_type=jnp.float32,
    )


def lookup(source, indices, first_row):
    position = indices - first_row
    inside = (position >= 0) & (position < source.shape[0])
    picked = jnp.take(source, jnp.clip(position, 0, source.shape[0] - 1), axis=0)
    return jnp.where(inside[:, None], picked, 0.0)


def any_draw(slab_embed, coverage_old, sel_index, cand_index):
    col_id = lax.axis_index("col")
    gathered = lax.all_gather(slab_embed, "row", axis=0, tiled=True)
    first_row = col_id * gathered.shape[0]
    selected, chosen = lax.psum(
        (lookup(gathered, sel_index, first_row), lookup(gathered, cand_index, first_row)), "col"
    )
    partial_value = jnp.max(similar(selected, gathered), axis=0)
    reached = lax.pmax(partial_value, "row")
    coverage = jnp.maximum(coverage_old, reached)
    gain_part = jnp.sum(jnp.maximum(similar(chosen, gathered) - coverage[None, :], 0.0), axis=1)
    return coverage, lax.psum(gain_part, "col")


def halves(value):
    high = value.astype(jnp.bfloat16)
    return high, (value - high.astype(jnp.float32)).astype(jnp.bfloat16)


def dot(left, right):
    return jnp.dot(left, right, preferred_element_type=jnp.float32)


def dot_nt(left, right):
    return lax.dot_general(left, right, NT, preferred_element_type=jnp.float32)


def kernel(
    R, C, cap, sent, slab, cov_old, sel, cand,
    cov_out, gain_out, flag_out,
    pts, ph, plo, qs, qh, ql, sc, idx, bias, best, mx, cov, gr,
    idx_send, idx_recv, core_send, core_recv, x_send, x_recv, f_send, f_recv,
    q_recv, ql_send, qr_send, qa_send, t_send, t_recv, m_send, m_recv, c_send, c_recv, g_send, g_recv,
):
    A = R // QUAD
    NB = A * C
    ND = R * C
    rows = slab.shape[0]
    ns, nk = sel.shape[1], cand.shape[1]
    shift = rows.bit_length() - 1
    span = QUAD * rows
    r = lax.axis_index("row")
    c = lax.axis_index("col")
    me = c * R + r
    a = lax.div(r, QUAD)
    m = lax.rem(r, QUAD)
    x, h = lax.div(m, 2), lax.rem(m, 2)
    m_core = 2 * x + (1 - h)
    m_x = 2 * (1 - x) + h
    m_diag = 2 * (1 - x) + (1 - h)
    base = a * QUAD
    width = 256
    parts = rows // width

    def remote(src, dst, ssem, rsem, row, col):
        return pltpu.make_async_remote_copy(
            src_ref=src, dst_ref=dst, send_sem=ssem, recv_sem=rsem,
            device_id=(row, col), device_id_type=MESH,
        )

    barrier = pltpu.get_barrier_semaphore()

    def others(act):
        def wrap(value, size):
            return jnp.where(value >= size, value - size, value)

        for dr in range(1, R):
            act(wrap(r + dr, R), c)

        def column(dc, carry):
            col = wrap(c + dc, C)
            for dr in range(R):
                act(wrap(r + dr, R), col)
            return carry

        lax.fori_loop(1, C, column, 0)

    others(
        lambda row, col: pl.semaphore_signal(barrier, inc=1, device_id=(row, col), device_id_type=MESH)
    )
    idx[r] = jnp.full(idx.shape[1:], -1, jnp.int32)
    idx[r, :, 0:ns] = sel[...]
    idx[r, :, ns : ns + nk] = cand[...]
    pl.semaphore_wait(barrier, ND - 1)

    def idx_copy(slot, to):
        return remote(idx.at[slot], idx.at[slot], idx_send.at[to], idx_recv.at[slot], to, c)

    for i in range(1, R):
        idx_copy(r, lax.rem(r + i, R)).start()

    core_copy = remote(slab, pts.at[m], core_send.at[0], core_recv.at[0], base + m_core, c)
    core_copy.start()

    half = width // 2

    def x_copy(s):
        part = pl.ds(s * half, half)
        return remote(slab.at[part], pts.at[m, part], x_send.at[s], x_recv.at[s], base + m_x, c)

    def x_landed(s):
        part = pl.ds(s * half, half)
        return remote(slab.at[part], pts.at[m_x, part], x_send.at[s], x_recv.at[s], base + m_x, c)

    def f_copy(s):
        part = pl.ds(s * width, width)
        return remote(pts.at[m_x, part], pts.at[m_x, part], f_send.at[s], f_recv.at[s], base + m_core, c)

    def f_landed(s):
        part = pl.ds(s * width, width)
        return remote(pts.at[m_diag, part], pts.at[m_diag, part], f_send.at[s], f_recv.at[s], base + m_core, c)

    for s in range(parts):
        x_copy(s).start()

    def split_part(source, slot, s):
        part = pl.ds(s * width, width)
        high, low = halves(source[part].T)
        ph[slot, s] = high
        plo[slot, s] = low

    def split_points(source, slot):
        for s in range(parts):
            split_part(source, slot, s)

    if sent < cap:
        qs[:, sent:] = jnp.zeros((NB, cap - sent, qs.shape[2]), jnp.float32)
    best[...] = jnp.full(best.shape, -1e30, jnp.float32)
    split_points(slab, m)

    for i in range(1, R):
        idx_copy(lax.rem(r + i, R), lax.rem(r + i, R)).wait_recv()

    everything = jnp.concatenate([idx[j] for j in range(R)], axis=0)
    owner = lax.shift_right_logical(everything, shift)
    local = (everything - owner * rows).astype(jnp.float32)
    owner_sel, owner_cand = owner[:, 0:ns], owner[:, ns:]
    slot_id = lax.broadcasted_iota(jnp.int32, (cap, 128), 0).astype(jnp.float32)

    def place(owners, locals_, start, packed):
        n = owners.shape[1]
        mask = jnp.where(owners == me, 1.0, 0.0)
        before = lax.broadcasted_iota(jnp.int32, (n, n), 0) < lax.broadcasted_iota(jnp.int32, (n, n), 1)
        within = jnp.dot(
            mask.astype(jnp.bfloat16), before.astype(jnp.bfloat16), preferred_element_type=jnp.float32
        )
        for j in range(R):
            rank = jnp.where(mask[j : j + 1] > 0.0, within[j : j + 1] + start, -1.0)
            spot = locals_[j : j + 1] + 1.0
            for lane in range(0, n, 128):
                packed = packed + jnp.where(
                    rank[:, lane : lane + 128] == slot_id, spot[:, lane : lane + 128], 0.0
                )
            start = start + jnp.sum(mask[j : j + 1], axis=1, keepdims=True)
        return start, packed

    start, packed = place(
        owner_sel, local[:, 0:ns], jnp.zeros((1, 1), jnp.float32), jnp.zeros((cap, 128), jnp.float32)
    )
    start, packed = place(owner_cand, local[:, ns:], start, packed)
    packed = jnp.sum(packed, axis=1, keepdims=True)
    point = lax.broadcasted_iota(jnp.int32, (cap, rows), 1).astype(jnp.float32)
    pick = jnp.where(point == packed - 1.0, 1.0, 0.0).astype(jnp.bfloat16)
    own = a * C + c
    rows_owned = jnp.zeros((cap, qs.shape[2]), jnp.float32)
    for s in range(parts):
        chosen = pick[:, s * width : (s + 1) * width]
        rows_owned = rows_owned + (dot_nt(chosen, ph[m, s]) + dot_nt(chosen, plo[m, s]))
    qs[own, 0:sent] = rows_owned[0:sent]

    last = jnp.where(2 * c < C, C - 1, 0)
    first = jnp.where(2 * c < C, 0, 1)
    inward = jnp.where(2 * c < C, 1, -1)
    head = -(-sent // 16) * 8

    def q_copy(b, ssem, row, col, start=0, size=sent):
        part = qs.at[b, pl.ds(start, size)]
        return remote(part, part, ssem.at[b], q_recv.at[b], row, col)

    def q_along(b, ssem, col):
        return q_copy(b, ssem, r, col)

    def q_across(b, i, size=sent):
        return q_copy(b, qa_send.at[i - 1], lax.rem(a + i, A) * QUAD + m, c, 0, size)

    def q_tail(i, col):
        part = qs.at[lax.rem(a + i, A) * C + last, pl.ds(head, sent - head)]
        return remote(part, part, t_send.at[i - 1, 0], t_recv.at[i - 1], r, col)

    def q_edge(i, edge, col):
        part = qs.at[lax.rem(a + i, A) * C + edge, pl.ds(head, sent - head)]
        return remote(part, part, t_send.at[i - 1, 1], t_recv.at[i - 1], r, col)

    def each_across(b, act):
        whole = b != a * C + last

        @pl.when(whole)
        def _():
            for i in range(1, A):
                act(q_across(b, i))

        @pl.when(jnp.logical_not(whole))
        def _():
            for i in range(1, A):
                act(q_across(b, i, head))

    def spread(b):
        each_across(b, lambda copy: copy.start())

    @pl.when(c + 1 < C)
    def _():
        q_along(own, qr_send, c + 1).start()

    @pl.when(c > 0)
    def _():
        q_along(own, ql_send, c - 1).start()

    spread(own)

    def split_block(b):
        high, low = halves(qs[b])
        qh[pl.ds(b * cap, cap)] = high
        ql[pl.ds(b * cap, cap)] = low

    def score(first, count, slot, s):
        out = pl.ds(slot * rows + s * width, width)
        block = pl.ds(first * cap, count * cap)
        high, low = ph[slot, s], plo[slot, s]
        n = count * cap
        both = dot(jnp.concatenate([qh[block], ql[block]], axis=0), high)
        value = both[0:n] + both[n:] + dot(qh[block], low)
        sc[block, out] = value
        shift_by = bias[block]
        top = jnp.concatenate(
            [
                jnp.max(
                    (value[:, lane : lane + 128] + shift_by).reshape(n // 8, 8, 128), axis=0
                )
                for lane in range(0, width, 128)
            ],
            axis=1,
        )
        best[:, out] = jnp.maximum(best[:, out], top)

    def near_scores(b):
        split_block(b)

        def step(t, carry):
            score(b, 1, 2 * x + lax.div(t, parts), lax.rem(t, parts))
            return carry

        lax.fori_loop(0, 2 * parts, step, 0)

    core_landed = remote(slab, pts.at[m_core], core_send.at[0], core_recv.at[0], base + m_core, c)
    core_landed.wait_recv()
    split_points(pts.at[m_core], m_core)
    def mark(b, carry):
        owner_id = lax.rem(b, C) * R + lax.div(b, C) * QUAD + m
        count = jnp.sum(
            jnp.sum(jnp.where(owner_sel == owner_id, 1.0, 0.0), axis=1, keepdims=True), axis=0, keepdims=True
        )
        bias[pl.ds(b * cap, cap)] = jnp.where(slot_id < count, 0.0, -1e30)
        return carry

    lax.fori_loop(0, NB, mark, 0)
    near_scores(own)

    square = (nk, nk)
    across, down = lax.broadcasted_iota(jnp.int32, square, 1), lax.broadcasted_iota(jnp.int32, square, 0)
    mine_row = lax.shift_right_logical(cand[...], shift).astype(jnp.float32)
    mine_owner = jnp.sum(jnp.where(across == down, mine_row, 0.0), axis=1, keepdims=True).astype(jnp.int32)
    wide = owner_cand.shape[1]
    earlier = lax.broadcasted_iota(jnp.int32, (nk, wide), 1) < lax.broadcasted_iota(jnp.int32, (nk, wide), 0)
    same_total = jnp.zeros((nk, 128), jnp.float32)
    for j in range(R):
        same = jnp.where(owner_sel[j : j + 1] == mine_owner, 1.0, 0.0)
        for lane in range(0, ns, 128):
            same_total = same_total + same[:, lane : lane + 128]
        counted = (j < r) | ((j == r) & earlier)
        same = jnp.where(counted & (owner_cand[j : j + 1] == mine_owner), 1.0, 0.0)
        for lane in range(0, wide, 128):
            same_total = same_total + same[:, lane : lane + 128]
    rank = jnp.sum(same_total, axis=1, keepdims=True)
    row_of = lax.rem(mine_owner, R)
    flat = lax.rem(row_of, QUAD) * NB + lax.div(row_of, QUAD) * C + lax.div(mine_owner, R)
    pick_owner = jnp.where(lax.broadcasted_iota(jnp.int32, (nk, ND), 1) == flat, 1.0, 0.0)
    pick_slot = lax.broadcasted_iota(jnp.int32, (nk, cap), 1).astype(jnp.float32) == rank

    dev_id = lax.broadcasted_iota(jnp.int32, (ND, 1), 0)
    held = jnp.zeros((ND, 128), jnp.float32)
    for j in range(R):
        for lane in range(0, ns + wide, 128):
            held = held + jnp.where(owner[j : j + 1, lane : lane + 128] == dev_id, 1.0, 0.0)
    held = jnp.sum(held, axis=1, keepdims=True)
    flag_out[...] = jnp.max(held, axis=0, keepdims=True)

    def arrive(b):
        q_copy(b, ql_send, r, c).wait_recv()

    inner = (c == C // 2) | (c == C // 2 - 1)

    def inside(col):
        return (col >= 0) & (col < C)

    def across_block(i, s, side):
        other = lax.rem(a + i, A) * C
        col = c + side * s

        @pl.when(inside(col) & (col != last))
        def _():
            arrive(other + col)

            @pl.when(inner & (s == C // 2 - 1) & (side != inward))
            def _():
                q_edge(i, C - 1 - last, c + inward).start()

            near_scores(other + col)

    def across_blocks(s):
        for i in range(1, A):
            across_block(i, s, -inward)

        @pl.when((s == C // 2 - 1) & (c > 0) & (c < C - 1))
        def _():
            for i in range(1, A):
                q_tail(i, c).wait_recv()
                q_tail(i, c - inward).start()

        @pl.when(s > 0)
        def _():
            for i in range(1, A):
                across_block(i, s, inward)

    def hand_on(s, side):
        @pl.when((s < C) & inside(c + side * s))
        def _():
            b = own + side * s
            arrive(b)

            @pl.when(inside(c - side))
            def _():
                q_along(b, ql_send, c - side).start()

            spread(b)

    def round_(s, carry):
        hand_on(s, -inward)
        hand_on(s, inward)

        def scores(k, carry):
            side = 2 * k - 1

            @pl.when((s < C) & inside(c + side * s))
            def _():
                near_scores(own + side * s)

            return carry

        lax.fori_loop(0, 2, scores, 0)

        @pl.when(s == 2)
        def _():
            for t in range(parts):
                x_landed(t).wait_recv()
            for t in range(parts // 2):
                f_copy(t).start()

        @pl.when(s == C - 1)
        def _():
            for t in range(parts, 2 * parts):
                x_landed(t).wait_recv()
            for t in range(parts // 2, parts):
                f_copy(t).start()

            def step(t, carry):
                split_part(pts.at[m_x], m_x, t)
                score(a * C, C, m_x, t)
                return carry

            lax.fori_loop(0, parts, step, 0)

        @pl.when(s == C)
        def _():
            for t in range(parts):
                f_landed(t).wait_recv()

            def step(t, carry):
                split_part(pts.at[m_diag], m_diag, t)
                score(a * C, C, m_diag, t)
                return carry

            lax.fori_loop(0, parts, step, 0)

        across_blocks(s - 1)

        @pl.when(s == 1)
        def _():
            for t in range(parts):
                x_copy(t).wait_send()
                x_copy(parts + t).start()

        return carry

    lax.fori_loop(1, C + 1, round_, 0)
    for i in range(1, A):
        other = lax.rem(a + i, A) * C

        def far_across(t, carry):
            score(other + first, C - 1, 2 * (1 - x) + lax.div(t, parts), lax.rem(t, parts))
            return carry

        lax.fori_loop(0, 2 * parts, far_across, 0)

    for i in range(1, A):
        other = lax.rem(a + i, A) * C
        q_copy(other + last, ql_send, r, c, 0, head).wait_recv()

        @pl.when((c == 0) | (c == C - 1))
        def _():
            q_tail(i, c).wait_recv()

        split_block(other + last)

        def last_scores(t, carry):
            score(other + last, 1, lax.div(t, parts), lax.rem(t, parts))
            return carry

        lax.fori_loop(0, QUAD * parts, last_scores, 0)

    mx[m] = jnp.max(best[...], axis=0, keepdims=True)

    def m_copy(slot, to):
        return remote(mx.at[slot], mx.at[slot], m_send.at[to], m_recv.at[slot], base + to, c)

    for i in range(1, QUAD):
        m_copy(m, lax.rem(m + i, QUAD)).start()
    for i in range(1, QUAD):
        m_copy(lax.rem(m + i, QUAD), lax.rem(m + i, QUAD)).wait_recv()
    reached = jnp.maximum(jnp.maximum(mx[0], mx[1]), jnp.maximum(mx[2], mx[3]))
    cov[a] = jnp.maximum(cov_old[a], reached)

    def c_copy(slot, to):
        return remote(cov.at[slot], cov.at[slot], c_send.at[to], c_recv.at[slot], to * QUAD + m, c)

    for i in range(1, A):
        c_copy(a, lax.rem(a + i, A)).start()

    mine = m * NB + own

    def gains(b, carry):
        total = jnp.zeros((cap, 128), jnp.float32)
        for part in range(0, span, 128):
            total = total + jnp.maximum(sc[pl.ds(b * cap, cap), part : part + 128] - cov[a, :, part : part + 128], 0.0)
        gr[mine, pl.ds(b, 1)] = jnp.sum(total.T, axis=0, keepdims=True)
        return carry

    lax.fori_loop(0, NB, gains, 0)

    def g_copy(part, row, col):
        return remote(part, part, g_send.at[0], g_recv.at[0], row, col)

    others(lambda row, col: g_copy(gr.at[mine], row, col).start())

    for i in range(1, A):
        c_copy(lax.rem(a + i, A), lax.rem(a + i, A)).wait_recv()
    cov_out[...] = cov[...]

    every = g_copy(gr.at[pl.ds(0, ND - 1)], r, c)
    every.wait_recv()
    totals = jnp.concatenate(
        [jnp.sum(gr[i * NB : (i + 1) * NB], axis=0) for i in range(QUAD)], axis=0
    )
    spread_gain = jnp.dot(pick_owner, totals, precision=lax.Precision.HIGHEST, preferred_element_type=jnp.float32)
    gain_out[...] = jnp.sum(jnp.where(pick_slot, spread_gain, 0.0), axis=1, keepdims=True)

    for i in range(1, R):
        idx_copy(r, lax.rem(r + i, R)).wait_send()
    core_copy.wait_send()

    for s in range(parts):
        x_copy(parts + s).wait_send()
        f_copy(s).wait_send()

    @pl.when(c + 1 < C)
    def _():
        q_along(own, qr_send, c + 1).wait_send()

    @pl.when(c > 0)
    def _():
        q_along(own, ql_send, c - 1).wait_send()

    each_across(own, lambda copy: copy.wait_send())

    @pl.when((c > 0) & (c < C - 1))
    def _():
        for i in range(1, A):
            q_tail(i, c - inward).wait_send()

    @pl.when(inner)
    def _():
        for i in range(1, A):
            q_edge(i, C - 1 - last, c + inward).wait_send()

    def left(s, carry):
        for side in (-1, 1):

            @pl.when(inside(c + side * s))
            def _():
                b = own + side * s

                @pl.when(inside(c - side))
                def _():
                    q_along(b, ql_send, c - side).wait_send()

                each_across(b, lambda copy: copy.wait_send())

        return carry

    lax.fori_loop(1, C, left, 0)
    for i in range(1, QUAD):
        m_copy(m, lax.rem(m + i, QUAD)).wait_send()
    for i in range(1, A):
        c_copy(a, lax.rem(a + i, A)).wait_send()

    every.wait_send()


def fused(R, C, slab_embed, coverage_old, sel_index, cand_index):
    rows, depth = slab_embed.shape
    ns, nk = sel_index.shape[0], cand_index.shape[0]
    A, ND = R // QUAD, R * C
    NB = A * C
    span = QUAD * rows
    mean = (ns + nk) * R / ND
    sent = int(-(-(mean + 3.7 * mean**0.5) // 8)) * 8
    cap = -(-sent // 32) * 32
    width = -(-(ns + nk) // 128) * 128
    parts = rows // 256
    f32, bf16, dma = jnp.float32, jnp.bfloat16, pltpu.SemaphoreType.DMA
    vmem = pl.BlockSpec(memory_space=pltpu.VMEM)
    coverage, gain, held = pl.pallas_call(
        functools.partial(kernel, R, C, cap, sent),
        out_shape=(
            jax.ShapeDtypeStruct((A, 1, span), f32),
            jax.ShapeDtypeStruct((nk, 1), f32),
            jax.ShapeDtypeStruct((1, 1), f32),
        ),
        in_specs=[vmem] * 4,
        out_specs=(vmem, vmem, vmem),
        scratch_shapes=[
            pltpu.VMEM((QUAD, rows, depth), f32),
            pltpu.VMEM((QUAD, parts, depth, 256), bf16),
            pltpu.VMEM((QUAD, parts, depth, 256), bf16),
            pltpu.VMEM((NB, cap, depth), f32),
            pltpu.VMEM((NB * cap, depth), bf16),
            pltpu.VMEM((NB * cap, depth), bf16),
            pltpu.VMEM((NB * cap, span), f32),
            pltpu.VMEM((R, 1, width), jnp.int32),
            pltpu.VMEM((NB * cap, 128), f32),
            pltpu.VMEM((8, span), f32),
            pltpu.VMEM((QUAD, 1, span), f32),
            pltpu.VMEM((A, 1, span), f32),
            pltpu.VMEM((ND, NB, cap), f32),
            dma((R,)), dma((R,)), dma((1,)), dma((1,)),
            dma((2 * parts,)), dma((2 * parts,)), dma((parts,)), dma((parts,)),
            dma((NB,)), dma((NB,)), dma((NB,)), dma((A - 1, NB)),
            dma((A - 1, 2)), dma((A - 1,)),
            dma((QUAD,)), dma((QUAD,)), dma((A,)), dma((A,)), dma((1,)), dma((1,)),
        ],
        compiler_params=pltpu.CompilerParams(
            collective_id=0, has_side_effects=True, vmem_limit_bytes=58 * 1024 * 1024
        ),
        cost_estimate=pl.CostEstimate(
            flops=6 * NB * cap * span * depth, bytes_accessed=rows * depth * 4, transcendentals=0
        ),
    )(
        slab_embed,
        coverage_old.reshape(A, 1, span),
        sel_index.reshape(1, ns),
        cand_index.reshape(1, nk),
    )
    return coverage.reshape(A * span), gain.reshape(nk), held[0, 0] > sent


def body(R, C, slab_embed, coverage_old, sel_index, cand_index):
    coverage, gain, crowded = fused(R, C, slab_embed, coverage_old, sel_index, cand_index)
    return lax.cond(
        crowded,
        lambda: any_draw(slab_embed, coverage_old, sel_index, cand_index),
        lambda: (coverage, gain),
    )


def solution(mesh):
    in_specs = (P(("col", "row"), None), P("col"), P("row"), P("row"))
    out_specs = (P("col"), P("row"))
    return jax.shard_map(
        functools.partial(body, mesh.shape["row"], mesh.shape["col"]),
        mesh=mesh, in_specs=in_specs, out_specs=out_specs, check_vma=False,
    )
```

```python
import functools

import jax
import jax.numpy as jnp
from jax import lax
from jax.experimental import pallas as pl
from jax.experimental.pallas import tpu as pltpu
from jax.sharding import PartitionSpec as P

MESH = pl.DeviceIdType.MESH
QUAD = 4
NT = (((1,), (1,)), ((), ()))


def similar(left, right):
    return lax.dot_general(
        left,
        right,
        (((1,), (1,)), ((), ())),
        precision=lax.Precision.HIGHEST,
        preferred_element_type=jnp.float32,
    )


def lookup(source, indices, first_row):
    position = indices - first_row
    inside = (position >= 0) & (position < source.shape[0])
    picked = jnp.take(source, jnp.clip(position, 0, source.shape[0] - 1), axis=0)
    return jnp.where(inside[:, None], picked, 0.0)


def any_draw(slab_embed, coverage_old, sel_index, cand_index):
    col_id = lax.axis_index("col")
    gathered = lax.all_gather(slab_embed, "row", axis=0, tiled=True)
    first_row = col_id * gathered.shape[0]
    selected, chosen = lax.psum(
        (lookup(gathered, sel_index, first_row), lookup(gathered, cand_index, first_row)), "col"
    )
    partial_value = jnp.max(similar(selected, gathered), axis=0)
    reached = lax.pmax(partial_value, "row")
    coverage = jnp.maximum(coverage_old, reached)
    gain_part = jnp.sum(jnp.maximum(similar(chosen, gathered) - coverage[None, :], 0.0), axis=1)
    return coverage, lax.psum(gain_part, "col")


def halves(value):
    high = value.astype(jnp.bfloat16)
    return high, (value - high.astype(jnp.float32)).astype(jnp.bfloat16)


def dot(left, right):
    return jnp.dot(left, right, preferred_element_type=jnp.float32)


def dot_nt(left, right):
    return lax.dot_general(left, right, NT, preferred_element_type=jnp.float32)


def kernel(
    R, C, cap, sent, slab, cov_old, sel, cand,
    cov_out, gain_out, flag_out,
    pts, ph, plo, qs, qh, ql, sc, idx, bias, best, mx, cov, gr,
    idx_send, idx_recv, core_send, core_recv, x_send, x_recv, f_send, f_recv,
    q_recv, ql_send, qr_send, qa_send, t_send, t_recv, m_send, m_recv, c_send, c_recv, g_send, g_recv,
):
    A = R // QUAD
    NB = A * C
    ND = R * C
    rows = slab.shape[0]
    ns, nk = sel.shape[1], cand.shape[1]
    shift = rows.bit_length() - 1
    span = QUAD * rows
    r = lax.axis_index("row")
    c = lax.axis_index("col")
    me = c * R + r
    a = lax.div(r, QUAD)
    m = lax.rem(r, QUAD)
    x, h = lax.div(m, 2), lax.rem(m, 2)
    m_core = 2 * x + (1 - h)
    m_x = 2 * (1 - x) + h
    m_diag = 2 * (1 - x) + (1 - h)
    base = a * QUAD
    width = 256
    parts = rows // width

    def remote(src, dst, ssem, rsem, row, col):
        return pltpu.make_async_remote_copy(
            src_ref=src, dst_ref=dst, send_sem=ssem, recv_sem=rsem,
            device_id=(row, col), device_id_type=MESH,
        )

    barrier = pltpu.get_barrier_semaphore()

    def others(act):
        def wrap(value, size):
            return jnp.where(value >= size, value - size, value)

        for dr in range(1, R):
            act(wrap(r + dr, R), c)

        def column(dc, carry):
            col = wrap(c + dc, C)
            for dr in range(R):
                act(wrap(r + dr, R), col)
            return carry

        lax.fori_loop(1, C, column, 0)

    others(
        lambda row, col: pl.semaphore_signal(barrier, inc=1, device_id=(row, col), device_id_type=MESH)
    )
    idx[r] = jnp.full(idx.shape[1:], -1, jnp.int32)
    idx[r, :, 0:ns] = sel[...]
    idx[r, :, ns : ns + nk] = cand[...]
    pl.semaphore_wait(barrier, ND - 1)

    def idx_copy(slot, to):
        return remote(idx.at[slot], idx.at[slot], idx_send.at[to], idx_recv.at[slot], to, c)

    for i in range(1, R):
        idx_copy(r, lax.rem(r + i, R)).start()

    core_copy = remote(slab, pts.at[m], core_send.at[0], core_recv.at[0], base + m_core, c)
    core_copy.start()

    half = width // 2

    def x_copy(s):
        part = pl.ds(s * half, half)
        return remote(slab.at[part], pts.at[m, part], x_send.at[s], x_recv.at[s], base + m_x, c)

    def x_landed(s):
        part = pl.ds(s * half, half)
        return remote(slab.at[part], pts.at[m_x, part], x_send.at[s], x_recv.at[s], base + m_x, c)

    def f_copy(s):
        part = pl.ds(s * width, width)
        return remote(pts.at[m_x, part], pts.at[m_x, part], f_send.at[s], f_recv.at[s], base + m_core, c)

    def f_landed(s):
        part = pl.ds(s * width, width)
        return remote(pts.at[m_diag, part], pts.at[m_diag, part], f_send.at[s], f_recv.at[s], base + m_core, c)

    for s in range(2 * parts):
        x_copy(s).start()

    def split_part(source, slot, s):
        part = pl.ds(s * width, width)
        high, low = halves(source[part].T)
        ph[slot, s] = high
        plo[slot, s] = low

    def split_points(source, slot):
        for s in range(parts):
            split_part(source, slot, s)

    if sent < cap:
        qs[:, sent:] = jnp.zeros((NB, cap - sent, qs.shape[2]), jnp.float32)
    best[...] = jnp.full(best.shape, -1e30, jnp.float32)
    split_points(slab, m)

    for i in range(1, R):
        idx_copy(lax.rem(r + i, R), lax.rem(r + i, R)).wait_recv()

    everything = jnp.concatenate([idx[j] for j in range(R)], axis=0)
    owner = lax.shift_right_logical(everything, shift)
    local = (everything - owner * rows).astype(jnp.float32)
    owner_sel, owner_cand = owner[:, 0:ns], owner[:, ns:]
    slot_id = lax.broadcasted_iota(jnp.int32, (cap, 128), 0).astype(jnp.float32)

    def place(owners, locals_, start, packed):
        n = owners.shape[1]
        mask = jnp.where(owners == me, 1.0, 0.0)
        before = lax.broadcasted_iota(jnp.int32, (n, n), 0) < lax.broadcasted_iota(jnp.int32, (n, n), 1)
        within = jnp.dot(
            mask.astype(jnp.bfloat16), before.astype(jnp.bfloat16), preferred_element_type=jnp.float32
        )
        for j in range(R):
            rank = jnp.where(mask[j : j + 1] > 0.0, within[j : j + 1] + start, -1.0)
            spot = locals_[j : j + 1] + 1.0
            for lane in range(0, n, 128):
                packed = packed + jnp.where(
                    rank[:, lane : lane + 128] == slot_id, spot[:, lane : lane + 128], 0.0
                )
            start = start + jnp.sum(mask[j : j + 1], axis=1, keepdims=True)
        return start, packed

    start, packed = place(
        owner_sel, local[:, 0:ns], jnp.zeros((1, 1), jnp.float32), jnp.zeros((cap, 128), jnp.float32)
    )
    start, packed = place(owner_cand, local[:, ns:], start, packed)
    packed = jnp.sum(packed, axis=1, keepdims=True)
    point = lax.broadcasted_iota(jnp.int32, (cap, rows), 1).astype(jnp.float32)
    pick = jnp.where(point == packed - 1.0, 1.0, 0.0).astype(jnp.bfloat16)
    own = a * C + c
    rows_owned = jnp.zeros((cap, qs.shape[2]), jnp.float32)
    for s in range(parts):
        chosen = pick[:, s * width : (s + 1) * width]
        rows_owned = rows_owned + (dot_nt(chosen, ph[m, s]) + dot_nt(chosen, plo[m, s]))
    qs[own, 0:sent] = rows_owned[0:sent]

    last = jnp.where(2 * c < C, C - 1, 0)
    first = jnp.where(2 * c < C, 0, 1)
    inward = jnp.where(2 * c < C, 1, -1)
    head = -(-sent // 16) * 8

    def q_copy(b, ssem, row, col, start=0, size=sent):
        part = qs.at[b, pl.ds(start, size)]
        return remote(part, part, ssem.at[b], q_recv.at[b], row, col)

    def q_along(b, ssem, col):
        return q_copy(b, ssem, r, col)

    def q_across(b, i, size=sent):
        return q_copy(b, qa_send.at[i - 1], lax.rem(a + i, A) * QUAD + m, c, 0, size)

    def q_tail(i, col):
        part = qs.at[lax.rem(a + i, A) * C + last, pl.ds(head, sent - head)]
        return remote(part, part, t_send.at[i - 1, 0], t_recv.at[i - 1], r, col)

    def q_edge(i, edge, col):
        part = qs.at[lax.rem(a + i, A) * C + edge, pl.ds(head, sent - head)]
        return remote(part, part, t_send.at[i - 1, 1], t_recv.at[i - 1], r, col)

    def each_across(b, act):
        whole = b != a * C + last

        @pl.when(whole)
        def _():
            for i in range(1, A):
                act(q_across(b, i))

        @pl.when(jnp.logical_not(whole))
        def _():
            for i in range(1, A):
                act(q_across(b, i, head))

    def spread(b):
        each_across(b, lambda copy: copy.start())

    @pl.when(c + 1 < C)
    def _():
        q_along(own, qr_send, c + 1).start()

    @pl.when(c > 0)
    def _():
        q_along(own, ql_send, c - 1).start()

    spread(own)

    def split_block(b):
        high, low = halves(qs[b])
        qh[pl.ds(b * cap, cap)] = high
        ql[pl.ds(b * cap, cap)] = low

    def score(first, count, slot, s):
        out = pl.ds(slot * rows + s * width, width)
        block = pl.ds(first * cap, count * cap)
        high, low = ph[slot, s], plo[slot, s]
        n = count * cap
        both = dot(jnp.concatenate([qh[block], ql[block]], axis=0), high)
        value = both[0:n] + both[n:] + dot(qh[block], low)
        sc[block, out] = value
        shift_by = bias[block]
        top = jnp.concatenate(
            [
                jnp.max(
                    (value[:, lane : lane + 128] + shift_by).reshape(n // 8, 8, 128), axis=0
                )
                for lane in range(0, width, 128)
            ],
            axis=1,
        )
        best[:, out] = jnp.maximum(best[:, out], top)

    def near_scores(b):
        split_block(b)

        def step(t, carry):
            score(b, 1, 2 * x + lax.div(t, parts), lax.rem(t, parts))
            return carry

        lax.fori_loop(0, 2 * parts, step, 0)

    core_landed = remote(slab, pts.at[m_core], core_send.at[0], core_recv.at[0], base + m_core, c)
    core_landed.wait_recv()
    split_points(pts.at[m_core], m_core)
    def mark(b, carry):
        owner_id = lax.rem(b, C) * R + lax.div(b, C) * QUAD + m
        count = jnp.sum(
            jnp.sum(jnp.where(owner_sel == owner_id, 1.0, 0.0), axis=1, keepdims=True), axis=0, keepdims=True
        )
        bias[pl.ds(b * cap, cap)] = jnp.where(slot_id < count, 0.0, -1e30)
        return carry

    lax.fori_loop(0, NB, mark, 0)
    near_scores(own)

    square = (nk, nk)
    across, down = lax.broadcasted_iota(jnp.int32, square, 1), lax.broadcasted_iota(jnp.int32, square, 0)
    mine_row = lax.shift_right_logical(cand[...], shift).astype(jnp.float32)
    mine_owner = jnp.sum(jnp.where(across == down, mine_row, 0.0), axis=1, keepdims=True).astype(jnp.int32)
    wide = owner_cand.shape[1]
    earlier = lax.broadcasted_iota(jnp.int32, (nk, wide), 1) < lax.broadcasted_iota(jnp.int32, (nk, wide), 0)
    same_total = jnp.zeros((nk, 128), jnp.float32)
    for j in range(R):
        same = jnp.where(owner_sel[j : j + 1] == mine_owner, 1.0, 0.0)
        for lane in range(0, ns, 128):
            same_total = same_total + same[:, lane : lane + 128]
        counted = (j < r) | ((j == r) & earlier)
        same = jnp.where(counted & (owner_cand[j : j + 1] == mine_owner), 1.0, 0.0)
        for lane in range(0, wide, 128):
            same_total = same_total + same[:, lane : lane + 128]
    rank = jnp.sum(same_total, axis=1, keepdims=True)
    row_of = lax.rem(mine_owner, R)
    flat = lax.rem(row_of, QUAD) * NB + lax.div(row_of, QUAD) * C + lax.div(mine_owner, R)
    pick_owner = jnp.where(lax.broadcasted_iota(jnp.int32, (nk, ND), 1) == flat, 1.0, 0.0)
    pick_slot = lax.broadcasted_iota(jnp.int32, (nk, cap), 1).astype(jnp.float32) == rank

    dev_id = lax.broadcasted_iota(jnp.int32, (ND, 1), 0)
    held = jnp.zeros((ND, 128), jnp.float32)
    for j in range(R):
        for lane in range(0, ns + wide, 128):
            held = held + jnp.where(owner[j : j + 1, lane : lane + 128] == dev_id, 1.0, 0.0)
    held = jnp.sum(held, axis=1, keepdims=True)
    flag_out[...] = jnp.max(held, axis=0, keepdims=True)

    def arrive(b):
        q_copy(b, ql_send, r, c).wait_recv()

    inner = (c == C // 2) | (c == C // 2 - 1)

    def inside(col):
        return (col >= 0) & (col < C)

    def across_block(i, s, side):
        other = lax.rem(a + i, A) * C
        col = c + side * s

        @pl.when(inside(col) & (col != last))
        def _():
            arrive(other + col)

            @pl.when(inner & (s == C // 2 - 1) & (side != inward))
            def _():
                q_edge(i, C - 1 - last, c + inward).start()

            near_scores(other + col)

    def across_blocks(s):
        for i in range(1, A):
            across_block(i, s, -inward)

        @pl.when((s == C // 2 - 1) & (c > 0) & (c < C - 1))
        def _():
            for i in range(1, A):
                q_tail(i, c).wait_recv()
                q_tail(i, c - inward).start()

        @pl.when(s > 0)
        def _():
            for i in range(1, A):
                across_block(i, s, inward)

    def hand_on(s, side):
        @pl.when((s < C) & inside(c + side * s))
        def _():
            b = own + side * s
            arrive(b)

            @pl.when(inside(c - side))
            def _():
                q_along(b, ql_send, c - side).start()

            spread(b)

    def round_(s, carry):
        hand_on(s, -inward)
        hand_on(s, inward)

        def scores(k, carry):
            side = 2 * k - 1

            @pl.when((s < C) & inside(c + side * s))
            def _():
                near_scores(own + side * s)

            return carry

        lax.fori_loop(0, 2, scores, 0)

        @pl.when(s == C - 1)
        def _():
            for t in range(parts):
                x_landed(2 * t).wait_recv()
                x_landed(2 * t + 1).wait_recv()
                f_copy(t).start()

            def step(t, carry):
                split_part(pts.at[m_x], m_x, t)
                score(a * C, C, m_x, t)
                return carry

            lax.fori_loop(0, parts, step, 0)

        @pl.when(s == C)
        def _():
            for t in range(parts):
                f_landed(t).wait_recv()

            def step(t, carry):
                split_part(pts.at[m_diag], m_diag, t)
                score(a * C, C, m_diag, t)
                return carry

            lax.fori_loop(0, parts, step, 0)

        across_blocks(s - 1)

        return carry

    lax.fori_loop(1, C + 1, round_, 0)
    for i in range(1, A):
        other = lax.rem(a + i, A) * C

        def far_across(t, carry):
            score(other + first, C - 1, 2 * (1 - x) + lax.div(t, parts), lax.rem(t, parts))
            return carry

        lax.fori_loop(0, 2 * parts, far_across, 0)

    for i in range(1, A):
        other = lax.rem(a + i, A) * C
        q_copy(other + last, ql_send, r, c, 0, head).wait_recv()

        @pl.when((c == 0) | (c == C - 1))
        def _():
            q_tail(i, c).wait_recv()

        split_block(other + last)

        def last_scores(t, carry):
            score(other + last, 1, lax.div(t, parts), lax.rem(t, parts))
            return carry

        lax.fori_loop(0, QUAD * parts, last_scores, 0)

    mx[m] = jnp.max(best[...], axis=0, keepdims=True)

    def m_copy(slot, to):
        return remote(mx.at[slot], mx.at[slot], m_send.at[to], m_recv.at[slot], base + to, c)

    for i in range(1, QUAD):
        m_copy(m, lax.rem(m + i, QUAD)).start()
    for i in range(1, QUAD):
        m_copy(lax.rem(m + i, QUAD), lax.rem(m + i, QUAD)).wait_recv()
    reached = jnp.maximum(jnp.maximum(mx[0], mx[1]), jnp.maximum(mx[2], mx[3]))
    cov[a] = jnp.maximum(cov_old[a], reached)

    def c_copy(slot, to):
        return remote(cov.at[slot], cov.at[slot], c_send.at[to], c_recv.at[slot], to * QUAD + m, c)

    for i in range(1, A):
        c_copy(a, lax.rem(a + i, A)).start()

    mine = m * NB + own

    def gains(b, carry):
        total = jnp.zeros((cap, 128), jnp.float32)
        for part in range(0, span, 128):
            total = total + jnp.maximum(sc[pl.ds(b * cap, cap), part : part + 128] - cov[a, :, part : part + 128], 0.0)
        gr[mine, pl.ds(b, 1)] = jnp.sum(total.T, axis=0, keepdims=True)
        return carry

    lax.fori_loop(0, NB, gains, 0)

    def g_copy(part, row, col):
        return remote(part, part, g_send.at[0], g_recv.at[0], row, col)

    others(lambda row, col: g_copy(gr.at[mine], row, col).start())

    for i in range(1, A):
        c_copy(lax.rem(a + i, A), lax.rem(a + i, A)).wait_recv()
    cov_out[...] = cov[...]

    every = g_copy(gr.at[pl.ds(0, ND - 1)], r, c)
    every.wait_recv()
    totals = jnp.concatenate(
        [jnp.sum(gr[i * NB : (i + 1) * NB], axis=0) for i in range(QUAD)], axis=0
    )
    spread_gain = jnp.dot(pick_owner, totals, precision=lax.Precision.HIGHEST, preferred_element_type=jnp.float32)
    gain_out[...] = jnp.sum(jnp.where(pick_slot, spread_gain, 0.0), axis=1, keepdims=True)

    for i in range(1, R):
        idx_copy(r, lax.rem(r + i, R)).wait_send()
    core_copy.wait_send()

    for s in range(parts):
        x_copy(2 * s).wait_send()
        x_copy(2 * s + 1).wait_send()
        f_copy(s).wait_send()

    @pl.when(c + 1 < C)
    def _():
        q_along(own, qr_send, c + 1).wait_send()

    @pl.when(c > 0)
    def _():
        q_along(own, ql_send, c - 1).wait_send()

    each_across(own, lambda copy: copy.wait_send())

    @pl.when((c > 0) & (c < C - 1))
    def _():
        for i in range(1, A):
            q_tail(i, c - inward).wait_send()

    @pl.when(inner)
    def _():
        for i in range(1, A):
            q_edge(i, C - 1 - last, c + inward).wait_send()

    def left(s, carry):
        for side in (-1, 1):

            @pl.when(inside(c + side * s))
            def _():
                b = own + side * s

                @pl.when(inside(c - side))
                def _():
                    q_along(b, ql_send, c - side).wait_send()

                each_across(b, lambda copy: copy.wait_send())

        return carry

    lax.fori_loop(1, C, left, 0)
    for i in range(1, QUAD):
        m_copy(m, lax.rem(m + i, QUAD)).wait_send()
    for i in range(1, A):
        c_copy(a, lax.rem(a + i, A)).wait_send()

    every.wait_send()


def fused(R, C, slab_embed, coverage_old, sel_index, cand_index):
    rows, depth = slab_embed.shape
    ns, nk = sel_index.shape[0], cand_index.shape[0]
    A, ND = R // QUAD, R * C
    NB = A * C
    span = QUAD * rows
    mean = (ns + nk) * R / ND
    sent = int(-(-(mean + 3.7 * mean**0.5) // 8)) * 8
    cap = -(-sent // 32) * 32
    width = -(-(ns + nk) // 128) * 128
    parts = rows // 256
    f32, bf16, dma = jnp.float32, jnp.bfloat16, pltpu.SemaphoreType.DMA
    vmem = pl.BlockSpec(memory_space=pltpu.VMEM)
    coverage, gain, held = pl.pallas_call(
        functools.partial(kernel, R, C, cap, sent),
        out_shape=(
            jax.ShapeDtypeStruct((A, 1, span), f32),
            jax.ShapeDtypeStruct((nk, 1), f32),
            jax.ShapeDtypeStruct((1, 1), f32),
        ),
        in_specs=[vmem] * 4,
        out_specs=(vmem, vmem, vmem),
        scratch_shapes=[
            pltpu.VMEM((QUAD, rows, depth), f32),
            pltpu.VMEM((QUAD, parts, depth, 256), bf16),
            pltpu.VMEM((QUAD, parts, depth, 256), bf16),
            pltpu.VMEM((NB, cap, depth), f32),
            pltpu.VMEM((NB * cap, depth), bf16),
            pltpu.VMEM((NB * cap, depth), bf16),
            pltpu.VMEM((NB * cap, span), f32),
            pltpu.VMEM((R, 1, width), jnp.int32),
            pltpu.VMEM((NB * cap, 128), f32),
            pltpu.VMEM((8, span), f32),
            pltpu.VMEM((QUAD, 1, span), f32),
            pltpu.VMEM((A, 1, span), f32),
            pltpu.VMEM((ND, NB, cap), f32),
            dma((R,)), dma((R,)), dma((1,)), dma((1,)),
            dma((2 * parts,)), dma((2 * parts,)), dma((parts,)), dma((parts,)),
            dma((NB,)), dma((NB,)), dma((NB,)), dma((A - 1, NB)),
            dma((A - 1, 2)), dma((A - 1,)),
            dma((QUAD,)), dma((QUAD,)), dma((A,)), dma((A,)), dma((1,)), dma((1,)),
        ],
        compiler_params=pltpu.CompilerParams(
            collective_id=0, has_side_effects=True, vmem_limit_bytes=58 * 1024 * 1024
        ),
        cost_estimate=pl.CostEstimate(
            flops=6 * NB * cap * span * depth, bytes_accessed=rows * depth * 4, transcendentals=0
        ),
    )(
        slab_embed,
        coverage_old.reshape(A, 1, span),
        sel_index.reshape(1, ns),
        cand_index.reshape(1, nk),
    )
    return coverage.reshape(A * span), gain.reshape(nk), held[0, 0] > sent


def body(R, C, slab_embed, coverage_old, sel_index, cand_index):
    coverage, gain, crowded = fused(R, C, slab_embed, coverage_old, sel_index, cand_index)
    return lax.cond(
        crowded,
        lambda: any_draw(slab_embed, coverage_old, sel_index, cand_index),
        lambda: (coverage, gain),
    )


def solution(mesh):
    in_specs = (P(("col", "row"), None), P("col"), P("row"), P("row"))
    out_specs = (P("col"), P("row"))
    return jax.shard_map(
        functools.partial(body, mesh.shape["row"], mesh.shape["col"]),
        mesh=mesh, in_specs=in_specs, out_specs=out_specs, check_vma=False,
    )
```
